32 devices in a mesh: ens: 2 (over x), lon: 16 (over z, y, core).
Axes of the slice: x: 2, y: 2, z: 4, core: 2. Of those that a mesh axis runs over, the one named last changes fastest.
Arguments:
- tracers: float32 [720, 32, 8, 128], P('lon', 'ens'), parts along dimension 1, may hold values from -6 to 6
- zonal_flux: float32 [64, 720, 128], P('ens', 'lon'), parts along dimension 0, may hold values from -0.3 to 0.3
- merid_flux: float32 [64, 720, 128], P('ens', 'lon'), parts along dimension 0, may hold values from -0.3 to 0.3
- kappa: float32 [128], replicated, may hold values from 0.1 to 100000
- levels: int32 [8], replicated, may hold values from 0 to 31
- groups: int32 [16], replicated, may hold values from 0 to 3
- emissions: float32 [4, 720, 128], P(None, 'lon'), may hold values from -4 to 8
- limiter: int32 [720, 128], P('lon'), may hold values 0 or 1
Outputs:
- updated: float32 [720, 32, 8, 128], P('lon', 'ens'), parts along dimension 1
The draws below stay inside these ranges and needn't reach their ends.
There are 2 independent parts, one for each index of `ens`. The reference program is written for one: setup_inputs(seed, part) draws one part's arguments, and reference() takes and returns one part's arrays. A program takes and returns all parts, laid end to end along the dimension named above; an argument that names none is the same for every part. Nothing has to cross between parts.
Inputs may be any that keep to these rules, and one draw needn't show every extreme that they name: Slab levels may repeat and need not be ordered.
All inputs are finite; a program needn't handle non-finite values. No bound on the sum of `limiter` on one device may be relied on, other than what follows from the above.
Results may differ from the reference program's by a relative error of at most 0.0012.
Values sent between devices are 32-bit elements; how exact they have to be, the bound alone decides.
A program may use at most 128 MiB of HBM per device.

```python
import math
import jax
import jax.numpy as jnp
from jax import lax

TRACERS = 16
GROUPS = 4
ARCH = 32
LEV = 8
NLAT = 128
NLON = 720


def draw_emissions(key, part):
    base = jax.random.fold_in(key, 7177)
    key_phase, key_level, key_rough = jax.random.split(base, 3)
    beside_all = jnp.arange(NLON, dtype=jnp.float32) * (2.0 * math.pi / NLON)
    phase = jax.random.uniform(key_phase, (GROUPS, 1, NLAT), jnp.float32, 0.0, 2.0 * math.pi)
    level = jax.random.uniform(key_level, (GROUPS, 1, NLAT), jnp.float32, 1.0, 2.5)
    rough = jnp.clip(jax.random.normal(key_rough, (GROUPS, NLON, NLAT), jnp.float32), -4.0, 4.0)
    smooth = level * (1.0 + 0.5 * jnp.cos(beside_all[None, :, None] + phase))
    return (smooth + rough).astype(jnp.float32)


def draw_kappa(key, part):
    base = jax.random.fold_in(key, 5113)
    key_order, key_jitter = jax.random.split(base, 2)
    order = jax.random.permutation(key_order, NLAT).astype(jnp.float32)
    jitter = jax.random.uniform(key_jitter, (NLAT,), jnp.float32, 0.0, 1.0)
    spread = jnp.maximum(NLAT - 1, 1)
    share = jnp.clip((order + jitter - 0.5) / spread, 0.0, 1.0)
    share = jnp.where(order == 0.0, 0.0, share)
    share = jnp.where(order == NLAT - 1.0, 1.0, share)
    return (10.0 ** (-1.0 + 6.0 * share)).astype(jnp.float32)


def touch_ends(result, own_key, low, top_value):
    longest = result.shape.index(max(result.shape))
    spots = []
    for shift in (0, 1):
        where = [jax.random.randint(jax.random.fold_in(own_key, axis), (), 0, length) for axis, length in enumerate(result.shape)]
        where[longest] = (where[longest] + shift) % result.shape[longest]
        spots.append(tuple(where))
    return result.at[spots[0]].set(low).at[spots[1]].set(top_value)


def level_of(key, extent, pieces, low, high):
    def one(axis_at, blocks):
        heights = jax.random.uniform(jax.random.fold_in(jax.random.fold_in(key, 6), axis_at), (blocks,), jnp.float32, low / len(pieces), high / len(pieces))
        return jnp.repeat(jnp.exp(heights), extent[axis_at] // blocks).reshape((-1,) + (1,) * (len(extent) - axis_at - 1))

    level = one(*pieces[0])
    for cut in pieces[1:]:
        level = level * one(*cut)
    return level


def bell_draw(rng, dims, scale, limit, pieces=(), kind=jnp.bfloat16):
    values = scale * jax.random.normal(rng, dims, jnp.float32)
    if pieces:
        values = values * level_of(rng, dims, pieces, -0.22, 0.18)
    return jnp.clip(values, -limit, limit).astype(kind)


def setup_inputs(seed: int = 0, part: int = 0) -> dict:
    keys = jax.random.split(jax.random.key(seed), 9)
    part_splits = jax.random.split(jax.random.fold_in(keys[8], part), 9)
    return {
        "tracers": bell_draw(part_splits[0], (NLON, TRACERS, LEV, NLAT), 1.0, 6.0, ((0, 16),), jnp.float32),
        "zonal_flux": jnp.clip(jax.random.uniform(part_splits[1], (ARCH, NLON, NLAT), jnp.float32, -0.3, 0.3) * level_of(part_splits[1], (ARCH, NLON, NLAT), ((1, 16),), -0.4, 0.0), -0.3, 0.3),
        "merid_flux": jnp.clip(jax.random.uniform(part_splits[2], (ARCH, NLON, NLAT), jnp.float32, -0.3, 0.3) * level_of(part_splits[2], (ARCH, NLON, NLAT), ((1, 16),), -0.4, 0.0), -0.3, 0.3),
        "kappa": draw_kappa(jax.random.fold_in(keys[8], 71), part),
        "levels": touch_ends(jax.random.randint(keys[4], (LEV,), 0, ARCH), jax.random.fold_in(keys[4], 1), 0, ARCH - 1).astype(jnp.int32),
        "groups": touch_ends(jax.random.randint(keys[5], (TRACERS,), 0, GROUPS), jax.random.fold_in(keys[5], 1), 0, GROUPS - 1).astype(jnp.int32),
        "emissions": draw_emissions(jax.random.fold_in(keys[8], 71), part),
        "limiter": touch_ends((jax.random.randint(keys[7], (NLON, NLAT), 0, 2) < 1).astype(jnp.int32), jax.random.fold_in(keys[7], 1), 0, 1),
    }


def thomas(lower_coef, diag_coef, upper_coef, right):
    def forward(carry, item):
        prev_ratio, prev_value = carry
        lower_here, diag_here, upper_here, right_here = item
        denom = diag_here - lower_here * prev_ratio
        ratio = upper_here / denom
        value = (right_here - lower_here * prev_value) / denom
        return (ratio, value), (ratio, value)

    start = (jnp.zeros_like(diag_coef[0]), jnp.zeros_like(right[0]))
    final_carry, (ratios, values) = lax.scan(forward, start, (lower_coef, diag_coef, upper_coef, right))

    def backward(later, item):
        ratio, value = item
        here = value - ratio * later
        return here, here

    last_carry, solved = lax.scan(backward, jnp.zeros_like(right[0]), (ratios, values), reverse=True)
    return solved


def meridional(tracers, north_face, limiter):
    south = jnp.roll(tracers, 1, axis=-1)
    face_flux = north_face[:, None]
    upwind = jnp.where(face_flux > 0, south, tracers)
    centered = 0.5 * (south + tracers)
    chosen = jnp.where(limiter[:, None, None, :] == 1, upwind, centered)
    rows = jnp.arange(tracers.shape[-1])
    flux = jnp.where(rows > 0, face_flux * chosen, 0.0)
    outgoing = jnp.where(rows < tracers.shape[-1] - 1, jnp.roll(flux, -1, axis=-1), 0.0)
    return flux - outgoing


def reference(tracers, zonal_flux, merid_flux, kappa, levels, groups, emissions, limiter):
    west = jnp.swapaxes(jnp.take(zonal_flux, levels, axis=0), 0, 1)[:, None]
    north_face = jnp.swapaxes(jnp.take(merid_flux, levels, axis=0), 0, 1)
    east = jnp.roll(west, -1, axis=0)
    lower_coef = -(west * 0.25 + kappa * 0.5)
    upper_coef = east * 0.25 - kappa * 0.5
    diag_coef = 1.0 + kappa + (east - west) * 0.25
    explicit = (2.0 - diag_coef) * tracers - lower_coef * jnp.roll(tracers, 1, axis=0) - upper_coef * jnp.roll(tracers, -1, axis=0)
    onehot = (groups[:, None] == jnp.arange(GROUPS, dtype=jnp.int32)[None, :]).astype(jnp.float32)
    source = jnp.einsum("tg,gij->itj", onehot, emissions, precision=lax.Precision.HIGHEST)[:, :, None, :]
    rhs = explicit + meridional(tracers, north_face, limiter) + source
    gamma = -diag_coef[0]
    alpha = upper_coef[-1]
    beta = lower_coef[0]
    diag_mod = diag_coef.at[0].set(diag_coef[0] - gamma)
    diag_mod = diag_mod.at[-1].set(diag_coef[-1] - alpha * beta / gamma)
    unit = jnp.zeros_like(diag_coef)
    unit = unit.at[0].set(gamma)
    unit = unit.at[-1].set(alpha)
    solved = thomas(lower_coef, diag_mod, upper_coef, jnp.concatenate([rhs, unit], axis=1))
    plain = solved[:, :TRACERS]
    spike = solved[:, TRACERS:]
    factor = (plain[0] + beta * plain[-1] / gamma) / (1.0 + spike[0] + beta * spike[-1] / gamma)
    return plain - factor[None] * spike
```

```python
import functools

import jax
import jax.numpy as jnp
from jax import lax
from jax.experimental import pallas as pl
from jax.experimental.pallas import tpu as pltpu
from jax.sharding import PartitionSpec as P

MESH = pl.DeviceIdType.MESH


def row(ref, index):
    return jnp.broadcast_to(ref[pl.ds(index, 1), :], (8, ref.shape[-1]))


def factor_units(n, kappa, coefs, back_s):
    half = kappa * 0.5

    def coef(d, c):
        return jnp.broadcast_to(coefs[d, pl.ds(c, 1), :], (8, kappa.shape[-1]))

    delta, z_prev = 1.0, 0.0
    ratios, zs = [], []
    for d in range(n):
        e = (d + 1) % n
        west = coef(e, 2)
        upper = west * 0.25 - half
        before = coef(d, 0)
        after = -upper * coef(e, 3)
        total = coef(d, 1) + west * 0.5 - upper * coef(e, 4)
        back_s[0, d] = upper
        if d < n - 1:
            num = total - before * delta
            inv = 1.0 / (num - after)
            delta = num * inv
            z_prev = total * inv - before * inv * z_prev
            back_s[1, d] = before * inv
            back_s[2, d] = inv
            ratio = after * inv
            back_s[3, d] = ratio
            ratios.append(ratio)
            zs.append(z_prev)
    for d in range(n - 3, -1, -1):
        zs[d] = zs[d] - ratios[d] * zs[d + 1]
    bottom = total - before * zs[n - 2] - after * zs[0]
    back_s[1, n - 1] = before
    back_s[2, n - 1] = 1.0 / bottom
    back_s[3, n - 1] = after
    for d in range(n - 1):
        back_s[4, d] = 1.0 - zs[d]


def solve_unit(n, back_s, gathered, solved):
    y_prev = 0.0
    ys = []
    for d in range(n):
        e = (d + 1) % n
        right = gathered[d, pl.ds(0, 8), :] - back_s[0, d] * gathered[e, pl.ds(8, 8), :]
        if d < n - 1:
            y_prev = right * back_s[2, d] - back_s[1, d] * y_prev
            ys.append(y_prev)
    for d in range(n - 3, -1, -1):
        ys[d] = ys[d] - back_s[3, d] * ys[d + 1]
    end = n - 1
    x_end = (right - back_s[1, end] * ys[end - 1] - back_s[3, end] * ys[0]) * back_s[2, end]
    solved[pl.ds(0, 8), :] = x_end
    solved[pl.ds(8 * n, 8), :] = x_end
    for d in range(n - 1):
        solved[pl.ds(8 * (d + 1), 8), :] = ys[d] + back_s[4, d] * x_end


def step_kernel(
    n,
    units,
    levels,
    groups,
    tracers_hbm,
    zonal_hbm,
    merid_hbm,
    kappa_ref,
    emissions_hbm,
    limiter_hbm,
    plain,
    w_ref,
    v_ref,
    out,
    tracers,
    zonal,
    merid,
    emissions,
    limiter,
    inv_s,
    low_s,
    ratio_s,
    g_s,
    p_s,
    q_s,
    c_s,
    c_message,
    message,
    coefs,
    gathered,
    back_s,
    solved,
    back,
    sem,
    s0,
    r0,
    s1,
    r1,
    s2,
    r2,
):
    cells, count, lev, lat = tracers.shape
    parts = count // 8
    last = cells - 1
    me = lax.axis_index("lon")
    ens = lax.axis_index("ens")
    every = n == units

    copies = [
        pltpu.make_async_copy(source, target, sem.at[at])
        for at, (source, target) in enumerate(
            (
                (zonal_hbm, zonal),
                (merid_hbm, merid),
                (emissions_hbm, emissions),
                (limiter_hbm, limiter),
                (tracers_hbm, tracers),
            )
        )
    ]
    for copy in copies:
        copy.start()
    barrier = pltpu.get_barrier_semaphore()

    def peer_of(step):
        return lax.rem(me + step, n)

    def source_of(step):
        return lax.rem(me + n - step, n)

    def when(condition):
        if every:
            return lambda f: f()
        return pl.when(condition)

    for step in range(1, n):
        pl.semaphore_signal(barrier, inc=1, device_id=(ens, peer_of(step)), device_id_type=MESH)

    def remote(source, target, send, recv, step):
        return pltpu.make_async_remote_copy(
            src_ref=source,
            dst_ref=target,
            send_sem=send.at[step],
            recv_sem=recv.at[step],
            device_id=(ens, peer_of(step)),
            device_id_type=MESH,
        )

    def early(step):
        return remote(c_message.at[peer_of(step)], coefs.at[me], s0, r0, step)

    def there(step):
        return remote(message.at[peer_of(step)], gathered.at[me], s1, r1, step)

    def home(step):
        return remote(
            solved.at[pl.ds(8 * peer_of(step), 16), :],
            back.at[pl.ds(16 * me, 16), :],
            s2,
            r2,
            step,
        )

    kappa = row(kappa_ref, 0)
    half = kappa * 0.5
    level = [levels[k] for k in range(lev)]
    group = [groups[t] for t in range(count)]
    lane = lax.broadcasted_iota(jnp.int32, (lev, lat), 1)
    sublane = lax.broadcasted_iota(jnp.int32, (lev, lat), 0)

    def at_cell(ref, i):
        value = jnp.broadcast_to(ref[i, pl.ds(level[0], 1), :], (lev, lat))
        for k in range(1, lev):
            other = jnp.broadcast_to(ref[i, pl.ds(level[k], 1), :], (lev, lat))
            value = jnp.where(sublane == k, other, value)
        return value

    def factor(i, carry):
        west, delta, w_prev, z_prev, g_here = carry
        east = at_cell(zonal, i + 1)
        lower = -(west * 0.25 + half)
        upper = east * 0.25 - half
        total = 1.0 + (east - west) * 0.5
        num = total - lower * delta
        inv = 1.0 / (num - upper)
        delta = num * inv
        low = lower * inv
        ratio = upper * inv
        w_here = -low * w_prev
        z_here = total * inv - low * z_prev
        inv_s[i] = inv
        low_s[i] = low
        ratio_s[i] = ratio
        g_s[i] = g_here
        w_ref[i] = w_here
        v_ref[i] = z_here
        return east, delta, w_here, z_here, -ratio * g_here

    copies[0].wait()
    west0 = at_cell(zonal, 0)
    ones = jnp.ones_like(west0)
    zeros = jnp.zeros_like(west0)
    west_last, _, w_last, z_last, _ = lax.fori_loop(
        0, last, factor, (west0, ones, -ones, zeros, ones), unroll=4
    )
    lower_last = -(west_last * 0.25 + half)

    def spikes(step, carry):
        i = last - 1 - step
        w_next, v_next, z_next = carry
        ratio = ratio_s[i]
        z_here = v_ref[i] - ratio * z_next
        w_here = w_ref[i] - ratio * w_next
        v_here = -ratio * v_next
        w_ref[i] = w_here
        v_ref[i] = v_here
        return w_here, v_here, z_here

    _, v_first, z_first = lax.fori_loop(0, last, spikes, (zeros, -ones, zeros), unroll=4)
    w_ref[last] = zeros
    v_ref[last] = -ones

    columns = (
        -lower_last * w_last,
        1.0 - west_last * 0.5 - lower_last * z_last,
        west0,
        v_first,
        z_first,
        zeros,
        zeros,
        zeros,
    )
    for at, column in enumerate(columns):
        c_s[pl.ds(8 * at, 8), :] = column
    for k in range(lev):
        for h in range(parts):
            c_message[k * parts + h] = c_s[pl.ds(k, 8, stride=8), :]
    for copy in copies[1:]:
        copy.wait()

    def rights(i):
        face = jnp.where(lane > 0, at_cell(merid, i), 0.0)
        upwind = jnp.where(face > 0, 1.0, 0.0)
        share = jnp.where(row(limiter, i) == 1, upwind, 0.5)
        south = face * share
        north = face * (1.0 - share)
        here = 2.0 + north - pltpu.roll(south, lat - 1, 1)
        after = -pltpu.roll(north, lat - 1, 1)
        result = []
        for t in range(count):
            value = tracers[i, t]
            source = jnp.broadcast_to(emissions[i, pl.ds(group[t], 1), :], (lev, lat))
            result.append(
                south * pltpu.roll(value, 1, 1)
                + here * value
                + (after * pltpu.roll(value, lat - 1, 1) + source)
            )
        return result

    def forward(i, carry):
        inv = inv_s[i]
        low = low_s[i]
        weight = g_s[i]
        values, firsts = [], []
        for t, right in enumerate(rights(i)):
            value = right * inv - low * carry[0][t]
            plain[i, t] = value
            values.append(value)
            firsts.append(carry[1][t] + weight * value)
        return tuple(values), tuple(firsts)

    ends, firsts = lax.fori_loop(
        0, last, forward, ((zeros,) * count, (zeros,) * count), unroll=2
    )
    for t, right in enumerate(rights(last)):
        p_s[pl.ds(t * lev, lev), :] = right - lower_last * ends[t]
        q_s[pl.ds(t * lev, lev), :] = firsts[t]
    for k in range(lev):
        for h in range(parts):
            unit = k * parts + h
            rows = pl.ds(h * 8 * lev + k, 8, stride=lev)
            message[unit, pl.ds(0, 8), :] = p_s[rows, :]
            message[unit, pl.ds(8, 8), :] = q_s[rows, :]
    pl.semaphore_wait(barrier, n - 1)
    for step in range(1, n):

        @when(peer_of(step) < units)
        def _():
            early(step).start()

    for step in range(1, n):

        @when(peer_of(step) < units)
        def _():
            there(step).start()

    @when(me < units)
    def _():
        coefs[me] = c_message[me]
        gathered[me] = message[me]
        for step in range(1, n):
            early(step).wait_recv()
        factor_units(n, kappa, coefs, back_s)

    def backward(step, carry):
        i = last - 1 - step
        ratio = ratio_s[i]
        result = []
        for t in range(count):
            value = plain[i, t] - ratio * carry[t]
            plain[i, t] = value - tracers[i, t]
            result.append(value)
        return tuple(result)

    lax.fori_loop(0, last, backward, (zeros,) * count, unroll=4)
    for t in range(count):
        plain[last, t] = -tracers[last, t]

    @when(me < units)
    def _():
        for step in range(1, n):
            there(step).wait_recv()
        solve_unit(n, back_s, gathered, solved)
        for step in range(1, n):
            home(step).start()
        back[pl.ds(16 * me, 16), :] = solved[pl.ds(8 * me, 16), :]

    for step in range(1, n):

        @when(peer_of(step) < units)
        def _():
            early(step).wait_send()
            there(step).wait_send()

    for step in range(1, n):

        @when(source_of(step) < units)
        def _():
            home(step).wait_recv()

    for j in range(2):
        for h in range(parts):
            for t in range(8):
                out[j, h * 8 + t] = back[pl.ds((h * 2 + j) * 8 + t, lev, stride=16 * parts), :]

    @when(me < units)
    def _():
        for step in range(1, n):
            home(step).wait_send()


def combine_kernel(cuts, plain, w_s, v_s, edges, out_hbm, buffer, done):
    count = buffer.shape[1]
    parts = [pl.ds(low, high - low) for low, high in zip(cuts[:-1], cuts[1:])]
    outs = [
        pltpu.make_async_copy(buffer.at[part], out_hbm.at[part], done.at[at])
        for at, part in enumerate(parts)
    ]

    def at_cell(i, carry):
        w_here, v_here = w_s[i], v_s[i]
        for t in range(count):
            buffer[i, t] = plain[i, t] - (w_here * edges[0, t] + v_here * edges[1, t])
        return carry

    for at in range(len(parts)):
        lax.fori_loop(cuts[at], cuts[at + 1], at_cell, 0, unroll=3)
        outs[at].start()
    for copy in outs:
        copy.wait()


def on_device(tracers, zonal_flux, merid_flux, kappa, levels, groups, emissions, limiter):
    n = lax.axis_size("lon")
    cells, count, lev, lat = tracers.shape
    units = lev * (count // 8)
    assert lev == 8 and count % 8 == 0 and n >= units
    f32 = jnp.float32
    hbm = pl.BlockSpec(memory_space=pl.ANY)
    vmem = pl.BlockSpec(memory_space=pltpu.VMEM)
    smem = pl.BlockSpec(memory_space=pltpu.SMEM)
    kappa = kappa.reshape(1, lat)
    zonal_flux, merid_flux, emissions = (
        jnp.swapaxes(value, 0, 1) for value in (zonal_flux, merid_flux, emissions)
    )
    column = (cells, lev, lat)
    levels, groups, tracers, zonal_flux, merid_flux, kappa, emissions, limiter = (
        pltpu.with_memory_space_constraint(value, pltpu.HBM)
        for value in (
            levels,
            groups,
            tracers,
            zonal_flux,
            merid_flux,
            kappa,
            emissions,
            limiter,
        )
    )
    plain, w_spike, v_spike, edges = pl.pallas_call(
        functools.partial(step_kernel, n, units),
        out_shape=(
            pltpu.VMEM(tracers.shape, f32),
            pltpu.VMEM(column, f32),
            pltpu.VMEM(column, f32),
            pltpu.VMEM((2, count, lev, lat), f32),
        ),
        in_specs=[smem, smem, hbm, hbm, hbm, vmem, hbm, hbm],
        out_specs=(vmem,) * 4,
        scratch_shapes=[
            pltpu.VMEM(tracers.shape, f32),
            pltpu.VMEM(zonal_flux.shape, f32),
            pltpu.VMEM(merid_flux.shape, f32),
            pltpu.VMEM(emissions.shape, f32),
            pltpu.VMEM(limiter.shape, jnp.int32),
        ]
        + [pltpu.VMEM(column, f32)] * 4
        + [
            pltpu.VMEM((count * lev, lat), f32),
            pltpu.VMEM((count * lev, lat), f32),
            pltpu.VMEM((64, lat), f32),
            pltpu.VMEM((units, 8, lat), f32),
            pltpu.VMEM((units, 16, lat), f32),
            pltpu.VMEM((n, 8, lat), f32),
            pltpu.VMEM((n, 16, lat), f32),
            pltpu.VMEM((5, n, 8, lat), f32),
            pltpu.VMEM((8 * (n + 1), lat), f32),
            pltpu.VMEM((units * 16, lat), f32),
            pltpu.SemaphoreType.DMA((5,)),
        ]
        + [pltpu.SemaphoreType.DMA((n,))] * 6,
        compiler_params=pltpu.CompilerParams(
            collective_id=0, has_side_effects=True, vmem_limit_bytes=32 << 20
        ),
        name="transport_step",
    )(levels, groups, tracers, zonal_flux, merid_flux, kappa, emissions, limiter)
    pieces = 5
    cuts = [cells * at // pieces for at in range(pieces + 1)]
    return pl.pallas_call(
        functools.partial(combine_kernel, cuts),
        out_shape=jax.ShapeDtypeStruct(tracers.shape, f32),
        in_specs=[vmem] * 4,
        out_specs=hbm,
        scratch_shapes=[
            pltpu.VMEM(tracers.shape, f32),
            pltpu.SemaphoreType.DMA((pieces,)),
        ],
        compiler_params=pltpu.CompilerParams(vmem_limit_bytes=32 << 20),
        name="combine",
    )(plain, w_spike, v_spike, edges)


def solution(mesh):
    placed = (
        P("lon", "ens", None, None),
        P("ens", "lon", None),
        P("ens", "lon", None),
        P(),
        P(),
        P(),
        P(None, "lon", None),
        P("lon", None),
    )
    return jax.shard_map(
        on_device,
        mesh=mesh,
        in_specs=placed,
        out_specs=P("lon", "ens", None, None),
        check_vma=False,
    )
```

```python
import functools

import jax
import jax.numpy as jnp
from jax import lax
from jax.experimental import pallas as pl
from jax.experimental.pallas import tpu as pltpu
from jax.sharding import PartitionSpec as P

MESH = pl.DeviceIdType.MESH


def row(ref, index):
    return jnp.broadcast_to(ref[pl.ds(index, 1), :], (8, ref.shape[-1]))


def factor_levels(n, kappa, coefs, back_s):
    half = kappa * 0.5

    def coef(d, c):
        return jnp.broadcast_to(coefs[d, pl.ds(c, 1), :], (8, kappa.shape[-1]))

    delta, z_prev = 1.0, 0.0
    ratios, zs = [], []
    for d in range(n):
        e = (d + 1) % n
        west = coef(e, 2)
        upper = west * 0.25 - half
        before = coef(d, 0)
        after = -upper * coef(e, 3)
        total = coef(d, 1) + west * 0.5 - upper * coef(e, 4)
        back_s[0, d] = upper
        if d < n - 1:
            num = total - before * delta
            inv = 1.0 / (num - after)
            delta = num * inv
            z_prev = total * inv - before * inv * z_prev
            back_s[1, d] = before * inv
            back_s[2, d] = inv
            ratio = after * inv
            back_s[3, d] = ratio
            ratios.append(ratio)
            zs.append(z_prev)
    for d in range(n - 3, -1, -1):
        zs[d] = zs[d] - ratios[d] * zs[d + 1]
    bottom = total - before * zs[n - 2] - after * zs[0]
    back_s[1, n - 1] = before
    back_s[2, n - 1] = 1.0 / bottom
    back_s[3, n - 1] = after
    for d in range(n - 1):
        back_s[4, d] = 1.0 - zs[d]


def solve_level(n, h, back_s, gathered, solved):
    y_prev = 0.0
    ys = []
    for d in range(n):
        e = (d + 1) % n
        right = gathered[h, d, pl.ds(0, 8), :] - back_s[0, d] * gathered[h, e, pl.ds(8, 8), :]
        if d < n - 1:
            y_prev = right * back_s[2, d] - back_s[1, d] * y_prev
            ys.append(y_prev)
    for d in range(n - 3, -1, -1):
        ys[d] = ys[d] - back_s[3, d] * ys[d + 1]
    end = n - 1
    x_end = (right - back_s[1, end] * ys[end - 1] - back_s[3, end] * ys[0]) * back_s[2, end]
    solved[h, pl.ds(0, 8), :] = x_end
    solved[h, pl.ds(8 * n, 8), :] = x_end
    for d in range(n - 1):
        solved[h, pl.ds(8 * (d + 1), 8), :] = ys[d] + back_s[4, d] * x_end


def step_kernel(
    n,
    first_owner,
    levels_hbm,
    groups_hbm,
    tracers_hbm,
    zonal_hbm,
    merid_hbm,
    kappa_hbm,
    emissions_hbm,
    limiter_hbm,
    plain,
    w_ref,
    v_ref,
    out,
    levels,
    groups,
    kappa_ref,
    tracers,
    zonal,
    merid,
    emissions,
    limiter,
    low_s,
    ratio_s,
    g_s,
    south_s,
    here_s,
    after_s,
    source_s,
    p_s,
    q_s,
    c_s,
    c_message,
    message,
    coefs,
    gathered,
    back_s,
    solved,
    back,
    sem,
    s0,
    r0,
    s1,
    r1,
    s2,
    r2,
):
    cells, count, lev, lat = tracers.shape
    kinds = emissions.shape[1]
    parts = count // 8
    last = cells - 1
    me = lax.axis_index("lon")
    ens = lax.axis_index("ens")
    is_owner = jnp.logical_and(me >= first_owner, me < first_owner + lev)
    mine = me - first_owner

    halves = [pl.ds(8 * h, 8) for h in range(parts)]
    copies = [
        pltpu.make_async_copy(source, target, sem.at[at])
        for at, (source, target) in enumerate(
            [
                (levels_hbm, levels),
                (kappa_hbm, kappa_ref),
                (zonal_hbm, zonal),
                (merid_hbm, merid),
                (limiter_hbm, limiter),
                (groups_hbm, groups),
                (emissions_hbm, emissions),
            ]
            + [(tracers_hbm.at[:, half], tracers.at[:, half]) for half in halves]
        )
    ]
    for copy in copies[:4]:
        copy.start()
    barrier = pltpu.get_barrier_semaphore()
    for k in range(lev):

        @pl.when(first_owner + k != me)
        def _():
            pl.semaphore_signal(
                barrier, inc=1, device_id=(ens, first_owner + k), device_id_type=MESH
            )

    @pl.when(is_owner)
    def _():
        for d in range(n):
            if d < first_owner or d >= first_owner + lev:
                pl.semaphore_signal(barrier, inc=1, device_id=(ens, d), device_id_type=MESH)

    for copy in copies[4:]:
        copy.start()

    def remote(source, target, send, recv, device):
        return pltpu.make_async_remote_copy(
            src_ref=source,
            dst_ref=target,
            send_sem=send,
            recv_sem=recv,
            device_id=(ens, device),
            device_id_type=MESH,
        )

    def early(k, sender):
        return remote(
            c_message.at[k], coefs.at[sender], s0.at[k], r0.at[sender], first_owner + k
        )

    def there(h, k, sender):
        return remote(
            message.at[h, k],
            gathered.at[h, sender],
            s1.at[h, k],
            r1.at[h, sender],
            first_owner + k,
        )

    def home(h, k, device):
        return remote(
            solved.at[h, pl.ds(8 * device, 16), :],
            back.at[h, pl.ds(16 * k, 16), :],
            s2.at[h, device],
            r2.at[h, k],
            device,
        )

    for copy in copies[:3]:
        copy.wait()
    kappa = row(kappa_ref, 0)
    half = kappa * 0.5
    level = [levels[k] for k in range(lev)]
    lane = lax.broadcasted_iota(jnp.int32, (lev, lat), 1)
    sublane = lax.broadcasted_iota(jnp.int32, (lev, lat), 0)

    def at_cell(ref, i):
        value = jnp.broadcast_to(ref[i, pl.ds(level[0], 1), :], (lev, lat))
        for k in range(1, lev):
            other = jnp.broadcast_to(ref[i, pl.ds(level[k], 1), :], (lev, lat))
            value = jnp.where(sublane == k, other, value)
        return value

    def prepare(i, inv):
        face = jnp.where(lane > 0, at_cell(merid, i), 0.0)
        upwind = jnp.where(face > 0, 1.0, 0.0)
        share = jnp.where(row(limiter, i) == 1, upwind, 0.5)
        south = face * share
        north = face - south
        south_s[i] = south * inv
        here_s[i] = (2.0 + north - pltpu.roll(south, lat - 1, 1)) * inv
        after_s[i] = pltpu.roll(north, lat - 1, 1) * inv
        for g in range(kinds):
            value = jnp.broadcast_to(emissions[i, pl.ds(g, 1), :], (lev, lat))
            source_s[i * kinds + g] = value * inv

    def factor(i, carry):
        west, delta, w_prev, z_prev, g_here, z_first = carry
        east = at_cell(zonal, i + 1)
        lower = -(west * 0.25 + half)
        upper = east * 0.25 - half
        total = 1.0 + (east - west) * 0.5
        num = total - lower * delta
        inv = 1.0 / (num - upper)
        delta = num * inv
        low = lower * inv
        ratio = upper * inv
        w_here = -low * w_prev
        z_here = total * inv - low * z_prev
        low_s[i] = low
        ratio_s[i] = ratio
        g_s[i] = g_here
        w_ref[i] = w_here
        prepare(i, inv)
        return east, delta, w_here, z_here, -ratio * g_here, z_first + g_here * z_here

    for copy in copies[3:7]:
        copy.wait()
    group = [groups[t] for t in range(count)]
    west0 = at_cell(zonal, 0)
    ones = jnp.ones_like(west0)
    zeros = jnp.zeros_like(west0)
    west_last, _, w_last, z_last, g_end, z_first = lax.fori_loop(
        0, last, factor, (west0, ones, -ones, zeros, ones, zeros), unroll=4
    )
    prepare(last, ones)
    lower_last = -(west_last * 0.25 + half)

    columns = (
        -lower_last * w_last,
        1.0 - west_last * 0.5 - lower_last * z_last,
        west0,
        -g_end,
        z_first,
        zeros,
        zeros,
        zeros,
    )
    for at, column in enumerate(columns):
        c_s[pl.ds(8 * at, 8), :] = column
    for k in range(lev):
        c_message[k] = c_s[pl.ds(k, 8, stride=8), :]

    def shifted(i, h):
        values = [tracers[i, 8 * h + t] for t in range(8)]
        return (
            tuple(pltpu.roll(value, 1, 1) for value in values),
            tuple(pltpu.roll(value, lat - 1, 1) for value in values),
        )

    def rights(h, i, souths, norths):
        south, here, after = south_s[i], here_s[i], after_s[i]
        return [
            south * souths[t]
            + here * tracers[i, 8 * h + t]
            + (source_s[i * kinds + group[8 * h + t]] - after * norths[t])
            for t in range(8)
        ]

    def forward(h, i, carry):
        before, sums, souths, norths = carry
        low, weight = low_s[i], g_s[i]
        values, firsts = [], []
        for t, right in enumerate(rights(h, i, souths, norths)):
            value = right - low * before[t]
            plain[i, 8 * h + t] = value
            values.append(value)
            firsts.append(sums[t] + weight * value)
        return (tuple(values), tuple(firsts), *shifted(i + 1, h))

    def sweep(h):
        copies[7 + h].wait()
        nothing = (zeros,) * 8
        ends, firsts, souths, norths = lax.fori_loop(
            0, last, functools.partial(forward, h), (nothing, nothing, *shifted(0, h)), unroll=4
        )
        for t, right in enumerate(rights(h, last, souths, norths)):
            p_s[pl.ds(t * lev, lev), :] = right - lower_last * ends[t]
            q_s[pl.ds(t * lev, lev), :] = firsts[t]
        for k in range(lev):
            rows = pl.ds(k, 8, stride=lev)
            message[h, k, pl.ds(0, 8), :] = p_s[rows, :]
            message[h, k, pl.ds(8, 8), :] = q_s[rows, :]

    def send(copy_of):
        for k in range(lev):

            @pl.when(first_owner + k != me)
            def _():
                copy_of(k).start()

    for h in range(parts):
        sweep(h)
        if h == 0:

            @pl.when(is_owner)
            def _():
                pl.semaphore_wait(barrier, n - 1)

            @pl.when(jnp.logical_not(is_owner))
            def _():
                pl.semaphore_wait(barrier, lev)

            send(lambda k: early(k, me))
            for g in range(h):
                send(lambda k: there(g, k, me))
        if h >= 0:
            send(lambda k: there(h, k, me))

    @pl.when(is_owner)
    def _():
        coefs[me] = c_message[mine]
        for h in range(parts):
            gathered[h, me] = message[h, mine]

    def spikes(step, carry):
        i = last - 1 - step
        w_next, v_next = carry
        ratio = ratio_s[i]
        w_here = w_ref[i] - ratio * w_next
        v_here = -ratio * v_next
        w_ref[i] = w_here
        v_ref[i] = v_here
        return w_here, v_here

    lax.fori_loop(0, last, spikes, (zeros, -ones), unroll=4)
    w_ref[last] = zeros
    v_ref[last] = -ones

    def backward(step, carry):
        i = last - 1 - step
        ratio = ratio_s[i]
        result = []
        for t in range(count):
            value = plain[i, t] - ratio * carry[t]
            plain[i, t] = value - tracers[i, t]
            result.append(value)
        return tuple(result)

    lax.fori_loop(0, last, backward, (zeros,) * count, unroll=4)
    for t in range(count):
        plain[last, t] = -tracers[last, t]

    @pl.when(is_owner)
    def _():
        senders = [lax.rem(me + step, n) for step in range(1, n)]
        for d in senders:
            early(mine, d).wait_recv()
        factor_levels(n, kappa, coefs, back_s)
        for h in range(parts):
            for d in senders:
                there(h, mine, d).wait_recv()
            solve_level(n, h, back_s, gathered, solved)
            for d in senders:
                home(h, mine, d).start()
            back[h, pl.ds(16 * mine, 16), :] = solved[h, pl.ds(8 * me, 16), :]

    for h in range(parts):
        for k in range(lev):

            @pl.when(first_owner + k != me)
            def _():
                home(h, k, me).wait_recv()

        for j in range(2):
            for t in range(8):
                out[j, h * 8 + t] = back[h, pl.ds(j * 8 + t, lev, stride=16), :]

    for k in range(lev):

        @pl.when(first_owner + k != me)
        def _():
            early(k, me).wait_send()
            for h in range(parts):
                there(h, k, me).wait_send()

    @pl.when(is_owner)
    def _():
        for h in range(parts):
            for step in range(1, n):
                home(h, mine, lax.rem(me + step, n)).wait_send()


def combine_kernel(cuts, plain, w_s, v_s, edges, out_hbm, buffer, done):
    count = buffer.shape[1]
    parts = [pl.ds(low, high - low) for low, high in zip(cuts[:-1], cuts[1:])]
    outs = [
        pltpu.make_async_copy(buffer.at[part], out_hbm.at[part], done.at[at])
        for at, part in enumerate(parts)
    ]

    def at_cell(i, carry):
        w_here, v_here = w_s[i], v_s[i]
        for t in range(count):
            buffer[i, t] = plain[i, t] - (w_here * edges[0, t] + v_here * edges[1, t])
        return carry

    for at in range(len(parts)):
        lax.fori_loop(cuts[at], cuts[at + 1], at_cell, 0, unroll=3)
        outs[at].start()
    for copy in outs:
        copy.wait()


def on_device(tracers, zonal_flux, merid_flux, kappa, levels, groups, emissions, limiter):
    n = lax.axis_size("lon")
    cells, count, lev, lat = tracers.shape
    parts, kinds = count // 8, emissions.shape[0]
    first_owner = (n - lev) // 2
    assert lev == 8 and count % 8 == 0 and n >= lev
    f32 = jnp.float32
    hbm = pl.BlockSpec(memory_space=pl.ANY)
    vmem = pl.BlockSpec(memory_space=pltpu.VMEM)
    kappa = kappa.reshape(1, lat)
    zonal_flux, merid_flux, emissions = (
        jnp.swapaxes(value, 0, 1) for value in (zonal_flux, merid_flux, emissions)
    )
    column = (cells, lev, lat)
    levels, groups, tracers, zonal_flux, merid_flux, kappa, emissions, limiter = (
        pltpu.with_memory_space_constraint(value, pltpu.HBM)
        for value in (
            levels,
            groups,
            tracers,
            zonal_flux,
            merid_flux,
            kappa,
            emissions,
            limiter,
        )
    )
    plain, w_spike, v_spike, edges = pl.pallas_call(
        functools.partial(step_kernel, n, first_owner),
        out_shape=(
            pltpu.VMEM(tracers.shape, f32),
            pltpu.VMEM(column, f32),
            pltpu.VMEM(column, f32),
            pltpu.VMEM((2, count, lev, lat), f32),
        ),
        in_specs=[hbm] * 8,
        out_specs=(vmem,) * 4,
        scratch_shapes=[
            pltpu.SMEM(levels.shape, jnp.int32),
            pltpu.SMEM(groups.shape, jnp.int32),
            pltpu.VMEM(kappa.shape, f32),
            pltpu.VMEM(tracers.shape, f32),
            pltpu.VMEM(zonal_flux.shape, f32),
            pltpu.VMEM(merid_flux.shape, f32),
            pltpu.VMEM(emissions.shape, f32),
            pltpu.VMEM(limiter.shape, jnp.int32),
        ]
        + [pltpu.VMEM(column, f32)] * 6
        + [
            pltpu.VMEM((cells * kinds, lev, lat), f32),
            pltpu.VMEM((8 * lev, lat), f32),
            pltpu.VMEM((8 * lev, lat), f32),
            pltpu.VMEM((64, lat), f32),
            pltpu.VMEM((lev, 8, lat), f32),
            pltpu.VMEM((parts, lev, 16, lat), f32),
            pltpu.VMEM((n, 8, lat), f32),
            pltpu.VMEM((parts, n, 16, lat), f32),
            pltpu.VMEM((5, n, 8, lat), f32),
            pltpu.VMEM((parts, 8 * (n + 1), lat), f32),
            pltpu.VMEM((parts, 16 * lev, lat), f32),
            pltpu.SemaphoreType.DMA((7 + parts,)),
            pltpu.SemaphoreType.DMA((lev,)),
            pltpu.SemaphoreType.DMA((n,)),
            pltpu.SemaphoreType.DMA((parts, lev)),
            pltpu.SemaphoreType.DMA((parts, n)),
            pltpu.SemaphoreType.DMA((parts, n)),
            pltpu.SemaphoreType.DMA((parts, lev)),
        ],
        compiler_params=pltpu.CompilerParams(
            collective_id=0, has_side_effects=True, vmem_limit_bytes=32 << 20
        ),
        name="transport_step",
    )(levels, groups, tracers, zonal_flux, merid_flux, kappa, emissions, limiter)
    pieces = 5
    cuts = [cells * at // pieces for at in range(pieces + 1)]
    return pl.pallas_call(
        functools.partial(combine_kernel, cuts),
        out_shape=jax.ShapeDtypeStruct(tracers.shape, f32),
        in_specs=[vmem] * 4,
        out_specs=hbm,
        scratch_shapes=[
            pltpu.VMEM(tracers.shape, f32),
            pltpu.SemaphoreType.DMA((pieces,)),
        ],
        compiler_params=pltpu.CompilerParams(vmem_limit_bytes=32 << 20),
        name="combine",
    )(plain, w_spike, v_spike, edges)


def solution(mesh):
    placed = (
        P("lon", "ens", None, None),
        P("ens", "lon", None),
        P("ens", "lon", None),
        P(),
        P(),
        P(),
        P(None, "lon", None),
        P("lon", None),
    )
    return jax.shard_map(
        on_device,
        mesh=mesh,
        in_specs=placed,
        out_specs=P("lon", "ens", None, None),
        check_vma=False,
    )
```

```python
import functools

import jax
import jax.numpy as jnp
from jax import lax
from jax.experimental import pallas as pl
from jax.experimental.pallas import tpu as pltpu
from jax.sharding import PartitionSpec as P

MESH = pl.DeviceIdType.MESH


def row(ref, index):
    return jnp.broadcast_to(ref[pl.ds(index, 1), :], (8, ref.shape[-1]))


def factor_levels(n, kappa, coefs, back_s):
    half = kappa * 0.5

    def coef(d, c):
        return jnp.broadcast_to(coefs[d, pl.ds(c, 1), :], (8, kappa.shape[-1]))

    delta, z_prev = 1.0, 0.0
    ratios, zs = [], []
    for d in range(n):
        e = (d + 1) % n
        west = coef(e, 2)
        upper = west * 0.25 - half
        before = coef(d, 0)
        after = -upper * coef(e, 3)
        total = coef(d, 1) + west * 0.5 - upper * coef(e, 4)
        back_s[0, d] = upper
        if d < n - 1:
            num = total - before * delta
            inv = 1.0 / (num - after)
            delta = num * inv
            z_prev = total * inv - before * inv * z_prev
            back_s[1, d] = before * inv
            back_s[2, d] = inv
            ratio = after * inv
            back_s[3, d] = ratio
            ratios.append(ratio)
            zs.append(z_prev)
    for d in range(n - 3, -1, -1):
        zs[d] = zs[d] - ratios[d] * zs[d + 1]
    bottom = total - before * zs[n - 2] - after * zs[0]
    back_s[1, n - 1] = before
    back_s[2, n - 1] = 1.0 / bottom
    back_s[3, n - 1] = after
    for d in range(n - 1):
        back_s[4, d] = 1.0 - zs[d]


def solve_level(n, h, back_s, gathered, solved):
    y_prev = 0.0
    ys = []
    for d in range(n):
        e = (d + 1) % n
        right = gathered[h, d, pl.ds(0, 8), :] - back_s[0, d] * gathered[h, e, pl.ds(8, 8), :]
        if d < n - 1:
            y_prev = right * back_s[2, d] - back_s[1, d] * y_prev
            ys.append(y_prev)
    for d in range(n - 3, -1, -1):
        ys[d] = ys[d] - back_s[3, d] * ys[d + 1]
    end = n - 1
    x_end = (right - back_s[1, end] * ys[end - 1] - back_s[3, end] * ys[0]) * back_s[2, end]
    solved[h, pl.ds(0, 8), :] = x_end
    solved[h, pl.ds(8 * n, 8), :] = x_end
    for d in range(n - 1):
        solved[h, pl.ds(8 * (d + 1), 8), :] = ys[d] + back_s[4, d] * x_end


def step_kernel(
    n,
    first_owner,
    levels_hbm,
    groups_hbm,
    tracers_hbm,
    zonal_hbm,
    merid_hbm,
    kappa_hbm,
    emissions_hbm,
    limiter_hbm,
    plain,
    w_ref,
    v_ref,
    out,
    levels,
    groups,
    kappa_ref,
    tracers,
    zonal,
    merid,
    emissions,
    limiter,
    low_s,
    ratio_s,
    g_s,
    south_s,
    here_s,
    after_s,
    source_s,
    p_s,
    q_s,
    c_s,
    c_message,
    message,
    coefs,
    gathered,
    back_s,
    solved,
    back,
    sem,
    wave,
):
    cells, count, lev, lat = tracers.shape
    kinds = emissions.shape[1]
    parts = count // 8
    last = cells - 1
    me = lax.axis_index("lon")
    ens = lax.axis_index("ens")
    is_owner = jnp.logical_and(me >= first_owner, me < first_owner + lev)
    mine = me - first_owner

    halves = [pl.ds(8 * h, 8) for h in range(parts)]
    copies = [
        pltpu.make_async_copy(source, target, sem.at[at])
        for at, (source, target) in enumerate(
            [
                (levels_hbm, levels),
                (kappa_hbm, kappa_ref),
                (zonal_hbm, zonal),
                (merid_hbm, merid),
                (limiter_hbm, limiter),
                (groups_hbm, groups),
                (emissions_hbm, emissions),
            ]
            + [(tracers_hbm.at[:, half], tracers.at[:, half]) for half in halves]
        )
    ]
    for copy in copies[:4]:
        copy.start()
    barrier = pltpu.get_barrier_semaphore()

    def greet(device):
        pl.semaphore_signal(barrier, inc=1, device_id=(ens, device), device_id_type=MESH)

    @pl.when(is_owner)
    def _():
        for step in range(1, n):
            greet(lax.rem(me + step, n))

    @pl.when(jnp.logical_not(is_owner))
    def _():
        for k in range(lev):
            greet(first_owner + k)

    for copy in copies[4:]:
        copy.start()

    def remote(source, target, send, recv, device):
        return pltpu.make_async_remote_copy(
            src_ref=source,
            dst_ref=target,
            send_sem=send,
            recv_sem=recv,
            device_id=(ens, device),
            device_id_type=MESH,
        )

    def early(k, sender):
        return remote(
            c_message.at[k], coefs.at[sender], wave.at[0], wave.at[1], first_owner + k
        )

    def there(h, k, sender):
        return remote(
            message.at[h, k],
            gathered.at[h, sender],
            wave.at[2 + h],
            wave.at[2 + parts + h],
            first_owner + k,
        )

    def home(h, k, device):
        return remote(
            solved.at[h, pl.ds(8 * device, 16), :],
            back.at[h, pl.ds(16 * k, 16), :],
            wave.at[2 + 2 * parts + h],
            wave.at[2 + 3 * parts + h],
            device,
        )

    for copy in copies[:3]:
        copy.wait()
    kappa = row(kappa_ref, 0)
    half = kappa * 0.5
    level = [levels[k] for k in range(lev)]
    lane = lax.broadcasted_iota(jnp.int32, (lev, lat), 1)
    sublane = lax.broadcasted_iota(jnp.int32, (lev, lat), 0)

    def at_cell(ref, i):
        value = jnp.broadcast_to(ref[i, pl.ds(level[0], 1), :], (lev, lat))
        for k in range(1, lev):
            other = jnp.broadcast_to(ref[i, pl.ds(level[k], 1), :], (lev, lat))
            value = jnp.where(sublane == k, other, value)
        return value

    def prepare(i, inv):
        face = jnp.where(lane > 0, at_cell(merid, i), 0.0)
        upwind = jnp.where(face > 0, 1.0, 0.0)
        share = jnp.where(row(limiter, i) == 1, upwind, 0.5)
        south = face * share
        north = face - south
        south_s[i] = south * inv
        here_s[i] = (2.0 + north - pltpu.roll(south, lat - 1, 1)) * inv
        after_s[i] = pltpu.roll(north, lat - 1, 1) * inv
        for g in range(kinds):
            value = jnp.broadcast_to(emissions[i, pl.ds(g, 1), :], (lev, lat))
            source_s[i * kinds + g] = value * inv

    def factor(i, carry):
        west, delta, w_prev, z_prev, g_here, z_first = carry
        east = at_cell(zonal, i + 1)
        lower = -(west * 0.25 + half)
        upper = east * 0.25 - half
        total = 1.0 + (east - west) * 0.5
        num = total - lower * delta
        inv = 1.0 / (num - upper)
        delta = num * inv
        low = lower * inv
        ratio = upper * inv
        w_here = -low * w_prev
        z_here = total * inv - low * z_prev
        low_s[i] = low
        ratio_s[i] = ratio
        g_s[i] = g_here
        w_ref[i] = w_here
        prepare(i, inv)
        return east, delta, w_here, z_here, -ratio * g_here, z_first + g_here * z_here

    for copy in copies[3:7]:
        copy.wait()
    group = [groups[t] for t in range(count)]
    west0 = at_cell(zonal, 0)
    ones = jnp.ones_like(west0)
    zeros = jnp.zeros_like(west0)
    west_last, _, w_last, z_last, g_end, z_first = lax.fori_loop(
        0, last, factor, (west0, ones, -ones, zeros, ones, zeros), unroll=11
    )
    prepare(last, ones)
    lower_last = -(west_last * 0.25 + half)

    columns = (
        -lower_last * w_last,
        1.0 - west_last * 0.5 - lower_last * z_last,
        west0,
        -g_end,
        z_first,
        zeros,
        zeros,
        zeros,
    )
    for at, column in enumerate(columns):
        c_s[pl.ds(8 * at, 8), :] = column
    for k in range(lev):
        c_message[k] = c_s[pl.ds(k, 8, stride=8), :]

    def shifted(i, h):
        values = [tracers[i, 8 * h + t] for t in range(8)]
        return (
            tuple(pltpu.roll(value, 1, 1) for value in values),
            tuple(pltpu.roll(value, lat - 1, 1) for value in values),
        )

    def rights(h, i, souths, norths):
        south, here, after = south_s[i], here_s[i], after_s[i]
        return [
            south * souths[t]
            + here * tracers[i, 8 * h + t]
            + (source_s[i * kinds + group[8 * h + t]] - after * norths[t])
            for t in range(8)
        ]

    def forward(h, i, carry):
        before, sums, souths, norths = carry
        low, weight = low_s[i], g_s[i]
        values, firsts = [], []
        for t, right in enumerate(rights(h, i, souths, norths)):
            value = right - low * before[t]
            plain[i, 8 * h + t] = value
            values.append(value)
            firsts.append(sums[t] + weight * value)
        return (tuple(values), tuple(firsts), *shifted(i + 1, h))

    def sweep(h):
        copies[7 + h].wait()
        nothing = (zeros,) * 8
        ends, firsts, souths, norths = lax.fori_loop(
            0, last, functools.partial(forward, h), (nothing, nothing, *shifted(0, h)), unroll=22
        )
        for t, right in enumerate(rights(h, last, souths, norths)):
            p_s[pl.ds(t * lev, lev), :] = right - lower_last * ends[t]
            q_s[pl.ds(t * lev, lev), :] = firsts[t]
        for k in range(lev):
            rows = pl.ds(k, 8, stride=lev)
            message[h, k, pl.ds(0, 8), :] = p_s[rows, :]
            message[h, k, pl.ds(8, 8), :] = q_s[rows, :]

    def send(copy_of):
        @pl.when(is_owner)
        def _():
            for step in range(1, lev):
                copy_of(lax.rem(mine + step, lev)).start()

        @pl.when(jnp.logical_not(is_owner))
        def _():
            for k in range(lev):
                copy_of(k).start()

    def settle(block, at):
        pltpu.make_async_copy(block, block, wave.at[at]).wait()

    for h in range(parts):
        sweep(h)
        if h == 0:

            @pl.when(is_owner)
            def _():
                pl.semaphore_wait(barrier, n - 1)

            @pl.when(jnp.logical_not(is_owner))
            def _():
                pl.semaphore_wait(barrier, lev)

            send(lambda k: early(k, me))
            for g in range(h):
                send(lambda k: there(g, k, me))
        if h >= 0:
            send(lambda k: there(h, k, me))

    @pl.when(is_owner)
    def _():
        coefs[me] = c_message[mine]
        for h in range(parts):
            gathered[h, me] = message[h, mine]

    def spikes(step, carry):
        i = last - 1 - step
        w_next, v_next = carry
        ratio = ratio_s[i]
        w_here = w_ref[i] - ratio * w_next
        v_here = -ratio * v_next
        w_ref[i] = w_here
        v_ref[i] = v_here
        return w_here, v_here

    lax.fori_loop(0, last, spikes, (zeros, -ones), unroll=4)
    w_ref[last] = zeros
    v_ref[last] = -ones

    def backward(step, carry):
        i = last - 1 - step
        ratio = ratio_s[i]
        result = []
        for t in range(count):
            value = plain[i, t] - ratio * carry[t]
            plain[i, t] = value - tracers[i, t]
            result.append(value)
        return tuple(result)

    lax.fori_loop(0, last, backward, (zeros,) * count, unroll=4)
    for t in range(count):
        plain[last, t] = -tracers[last, t]

    @pl.when(is_owner)
    def _():
        others = pl.ds(0, n - 1)
        settle(coefs.at[others], 1)
        factor_levels(n, kappa, coefs, back_s)
        for h in range(parts):
            settle(gathered.at[h, others], 2 + parts + h)
            solve_level(n, h, back_s, gathered, solved)
            for step in range(n - 1):
                home(h, mine, step + jnp.where(step < me, 0, 1)).start()
            back[h, pl.ds(16 * mine, 16), :] = solved[h, pl.ds(8 * me, 16), :]

    def finish(h, owners):
        settle(back.at[h, pl.ds(0, 16 * owners)], 2 + 3 * parts + h)

    for h in range(parts):

        @pl.when(is_owner)
        def _():
            finish(h, lev - 1)

        @pl.when(jnp.logical_not(is_owner))
        def _():
            finish(h, lev)

        for j in range(2):
            for t in range(8):
                out[j, h * 8 + t] = back[h, pl.ds(j * 8 + t, lev, stride=16), :]

    def sent(owners):
        settle(c_message.at[pl.ds(0, owners)], 0)
        for h in range(parts):
            settle(message.at[h, pl.ds(0, owners)], 2 + h)

    @pl.when(is_owner)
    def _():
        sent(lev - 1)
        for h in range(parts):
            settle(gathered.at[h, pl.ds(0, n - 1)], 2 + 2 * parts + h)

    @pl.when(jnp.logical_not(is_owner))
    def _():
        sent(lev)


def combine_kernel(cuts, plain, w_s, v_s, edges, out_hbm, buffer, done):
    count = buffer.shape[1]
    parts = [pl.ds(low, high - low) for low, high in zip(cuts[:-1], cuts[1:])]
    outs = [
        pltpu.make_async_copy(buffer.at[part], out_hbm.at[part], done.at[at])
        for at, part in enumerate(parts)
    ]

    def at_cell(i, carry):
        w_here, v_here = w_s[i], v_s[i]
        for t in range(count):
            buffer[i, t] = plain[i, t] - (w_here * edges[0, t] + v_here * edges[1, t])
        return carry

    for at in range(len(parts)):
        lax.fori_loop(cuts[at], cuts[at + 1], at_cell, 0, unroll=3)
        outs[at].start()
    for copy in outs:
        copy.wait()


def on_device(tracers, zonal_flux, merid_flux, kappa, levels, groups, emissions, limiter):
    n = lax.axis_size("lon")
    cells, count, lev, lat = tracers.shape
    parts, kinds = count // 8, emissions.shape[0]
    first_owner = (n - lev) // 2
    assert lev == 8 and count % 8 == 0 and n >= lev
    f32 = jnp.float32
    hbm = pl.BlockSpec(memory_space=pl.ANY)
    vmem = pl.BlockSpec(memory_space=pltpu.VMEM)
    kappa = kappa.reshape(1, lat)
    zonal_flux, merid_flux, emissions = (
        jnp.swapaxes(value, 0, 1) for value in (zonal_flux, merid_flux, emissions)
    )
    column = (cells, lev, lat)
    levels, groups, tracers, zonal_flux, merid_flux, kappa, emissions, limiter = (
        pltpu.with_memory_space_constraint(value, pltpu.HBM)
        for value in (
            levels,
            groups,
            tracers,
            zonal_flux,
            merid_flux,
            kappa,
            emissions,
            limiter,
        )
    )
    plain, w_spike, v_spike, edges = pl.pallas_call(
        functools.partial(step_kernel, n, first_owner),
        out_shape=(
            pltpu.VMEM(tracers.shape, f32),
            pltpu.VMEM(column, f32),
            pltpu.VMEM(column, f32),
            pltpu.VMEM((2, count, lev, lat), f32),
        ),
        in_specs=[hbm] * 8,
        out_specs=(vmem,) * 4,
        scratch_shapes=[
            pltpu.SMEM(levels.shape, jnp.int32),
            pltpu.SMEM(groups.shape, jnp.int32),
            pltpu.VMEM(kappa.shape, f32),
            pltpu.VMEM(tracers.shape, f32),
            pltpu.VMEM(zonal_flux.shape, f32),
            pltpu.VMEM(merid_flux.shape, f32),
            pltpu.VMEM(emissions.shape, f32),
            pltpu.VMEM(limiter.shape, jnp.int32),
        ]
        + [pltpu.VMEM(column, f32)] * 6
        + [
            pltpu.VMEM((cells * kinds, lev, lat), f32),
            pltpu.VMEM((8 * lev, lat), f32),
            pltpu.VMEM((8 * lev, lat), f32),
            pltpu.VMEM((64, lat), f32),
            pltpu.VMEM((lev, 8, lat), f32),
            pltpu.VMEM((parts, lev, 16, lat), f32),
            pltpu.VMEM((n, 8, lat), f32),
            pltpu.VMEM((parts, n, 16, lat), f32),
            pltpu.VMEM((5, n, 8, lat), f32),
            pltpu.VMEM((parts, 8 * (n + 1), lat), f32),
            pltpu.VMEM((parts, 16 * lev, lat), f32),
            pltpu.SemaphoreType.DMA((7 + parts,)),
            pltpu.SemaphoreType.DMA((2 + 4 * parts,)),
        ],
        compiler_params=pltpu.CompilerParams(
            collective_id=0, has_side_effects=True, vmem_limit_bytes=32 << 20
        ),
        name="transport_step",
    )(levels, groups, tracers, zonal_flux, merid_flux, kappa, emissions, limiter)
    pieces = 5
    cuts = [cells * at // pieces for at in range(pieces + 1)]
    return pl.pallas_call(
        functools.partial(combine_kernel, cuts),
        out_shape=jax.ShapeDtypeStruct(tracers.shape, f32),
        in_specs=[vmem] * 4,
        out_specs=hbm,
        scratch_shapes=[
            pltpu.VMEM(tracers.shape, f32),
            pltpu.SemaphoreType.DMA((pieces,)),
        ],
        compiler_params=pltpu.CompilerParams(vmem_limit_bytes=32 << 20),
        name="combine",
    )(plain, w_spike, v_spike, edges)


def solution(mesh):
    placed = (
        P("lon", "ens", None, None),
        P("ens", "lon", None),
        P("ens", "lon", None),
        P(),
        P(),
        P(),
        P(None, "lon", None),
        P("lon", None),
    )
    return jax.shard_map(
        on_device,
        mesh=mesh,
        in_specs=placed,
        out_specs=P("lon", "ens", None, None),
        check_vma=False,
    )
```

```python
import functools

import jax
import jax.numpy as jnp
from jax import lax
from jax.experimental import pallas as pl
from jax.experimental.pallas import tpu as pltpu
from jax.sharding import PartitionSpec as P

MESH = pl.DeviceIdType.MESH


def row(ref, index):
    return jnp.broadcast_to(ref[pl.ds(index, 1), :], (8, ref.shape[-1]))


def factor_levels(n, kappa, coefs, back_s):
    half = kappa * 0.5

    def coef(d, c):
        return jnp.broadcast_to(coefs[d, pl.ds(c, 1), :], (8, kappa.shape[-1]))

    delta, z_prev = 1.0, 0.0
    ratios, zs = [], []
    for d in range(n):
        e = (d + 1) % n
        west = coef(e, 2)
        upper = west * 0.25 - half
        before = coef(d, 0)
        after = -upper * coef(e, 3)
        total = coef(d, 1) + west * 0.5 - upper * coef(e, 4)
        back_s[0, d] = upper
        if d < n - 1:
            num = total - before * delta
            inv = 1.0 / (num - after)
            delta = num * inv
            z_prev = total * inv - before * inv * z_prev
            back_s[1, d] = before * inv
            back_s[2, d] = inv
            ratio = after * inv
            back_s[3, d] = ratio
            ratios.append(ratio)
            zs.append(z_prev)
    for d in range(n - 3, -1, -1):
        zs[d] = zs[d] - ratios[d] * zs[d + 1]
    bottom = total - before * zs[n - 2] - after * zs[0]
    back_s[1, n - 1] = before
    back_s[2, n - 1] = 1.0 / bottom
    back_s[3, n - 1] = after
    for d in range(n - 1):
        back_s[4, d] = 1.0 - zs[d]


def solve_level(n, h, back_s, gathered, solved):
    y_prev = 0.0
    ys = []
    for d in range(n):
        e = (d + 1) % n
        right = gathered[h, d, pl.ds(0, 8), :] - back_s[0, d] * gathered[h, e, pl.ds(8, 8), :]
        if d < n - 1:
            y_prev = right * back_s[2, d] - back_s[1, d] * y_prev
            ys.append(y_prev)
    for d in range(n - 3, -1, -1):
        ys[d] = ys[d] - back_s[3, d] * ys[d + 1]
    end = n - 1
    x_end = (right - back_s[1, end] * ys[end - 1] - back_s[3, end] * ys[0]) * back_s[2, end]
    solved[h, pl.ds(0, 8), :] = x_end
    solved[h, pl.ds(8 * n, 8), :] = x_end
    for d in range(n - 1):
        solved[h, pl.ds(8 * (d + 1), 8), :] = ys[d] + back_s[4, d] * x_end


def step_kernel(
    n,
    first_owner,
    levels_hbm,
    groups_hbm,
    tracers_hbm,
    zonal_hbm,
    merid_hbm,
    kappa_hbm,
    emissions_hbm,
    limiter_hbm,
    plain,
    w_ref,
    v_ref,
    out,
    levels,
    groups,
    kappa_ref,
    tracers,
    zonal,
    merid,
    emissions,
    limiter,
    low_s,
    ratio_s,
    g_s,
    south_s,
    here_s,
    after_s,
    source_s,
    p_s,
    q_s,
    c_s,
    c_message,
    message,
    coefs,
    gathered,
    back_s,
    solved,
    back,
    sem,
    wave,
):
    cells, count, lev, lat = tracers.shape
    kinds = emissions.shape[1]
    parts = count // 8
    last = cells - 1
    me = lax.axis_index("lon")
    ens = lax.axis_index("ens")
    is_owner = jnp.logical_and(me >= first_owner, me < first_owner + lev)
    mine = me - first_owner

    halves = [pl.ds(8 * h, 8) for h in range(parts)]
    copies = [
        pltpu.make_async_copy(source, target, sem.at[at])
        for at, (source, target) in enumerate(
            [
                (levels_hbm, levels),
                (kappa_hbm, kappa_ref),
                (zonal_hbm, zonal),
                (merid_hbm, merid),
                (limiter_hbm, limiter),
                (groups_hbm, groups),
                (emissions_hbm, emissions),
            ]
            + [(tracers_hbm.at[:, half], tracers.at[:, half]) for half in halves]
        )
    ]
    for copy in copies[:4]:
        copy.start()
    barrier = pltpu.get_barrier_semaphore()

    def greet(device):
        pl.semaphore_signal(barrier, inc=1, device_id=(ens, device), device_id_type=MESH)

    @pl.when(is_owner)
    def _():
        for step in range(1, n):
            greet(lax.rem(me + step, n))

    @pl.when(jnp.logical_not(is_owner))
    def _():
        for k in range(lev):
            greet(first_owner + k)

    for copy in copies[4:]:
        copy.start()

    def remote(source, target, send, recv, device):
        return pltpu.make_async_remote_copy(
            src_ref=source,
            dst_ref=target,
            send_sem=send,
            recv_sem=recv,
            device_id=(ens, device),
            device_id_type=MESH,
        )

    def early(k, sender):
        return remote(
            c_message.at[k], coefs.at[sender], wave.at[0], wave.at[1], first_owner + k
        )

    def there(h, k, sender):
        return remote(
            message.at[h, k],
            gathered.at[h, sender],
            wave.at[2 + h],
            wave.at[2 + parts + h],
            first_owner + k,
        )

    def home(h, k, device):
        return remote(
            solved.at[h, pl.ds(8 * device, 16), :],
            back.at[h, pl.ds(16 * k, 16), :],
            wave.at[2 + 2 * parts + h],
            wave.at[2 + 3 * parts + h],
            device,
        )

    for copy in copies[:3]:
        copy.wait()
    kappa = row(kappa_ref, 0)
    half = kappa * 0.5
    level = [levels[k] for k in range(lev)]
    lane = lax.broadcasted_iota(jnp.int32, (lev, lat), 1)
    sublane = lax.broadcasted_iota(jnp.int32, (lev, lat), 0)

    def at_cell(ref, i):
        value = jnp.broadcast_to(ref[i, pl.ds(level[0], 1), :], (lev, lat))
        for k in range(1, lev):
            other = jnp.broadcast_to(ref[i, pl.ds(level[k], 1), :], (lev, lat))
            value = jnp.where(sublane == k, other, value)
        return value

    def prepare(i, inv):
        face = jnp.where(lane > 0, at_cell(merid, i), 0.0)
        upwind = jnp.where(face > 0, 1.0, 0.0)
        share = jnp.where(row(limiter, i) == 1, upwind, 0.5)
        south = face * share
        north = face - south
        south_s[i] = south * inv
        here_s[i] = (2.0 + north - pltpu.roll(south, lat - 1, 1)) * inv
        after_s[i] = pltpu.roll(north, lat - 1, 1) * inv
        for g in range(kinds):
            value = jnp.broadcast_to(emissions[i, pl.ds(g, 1), :], (lev, lat))
            source_s[i * kinds + g] = value * inv

    def factor(i, carry):
        west, delta, w_prev, z_prev, g_here, z_first = carry
        east = at_cell(zonal, i + 1)
        lower = -(west * 0.25 + half)
        upper = east * 0.25 - half
        total = 1.0 + (east - west) * 0.5
        num = total - lower * delta
        inv = 1.0 / (num - upper)
        delta = num * inv
        low = lower * inv
        ratio = upper * inv
        w_here = -low * w_prev
        z_here = total * inv - low * z_prev
        low_s[i] = low
        ratio_s[i] = ratio
        g_s[i] = g_here
        w_ref[i] = w_here
        prepare(i, inv)
        return east, delta, w_here, z_here, -ratio * g_here, z_first + g_here * z_here

    for copy in copies[3:7]:
        copy.wait()
    group = [groups[t] for t in range(count)]
    west0 = at_cell(zonal, 0)
    ones = jnp.ones_like(west0)
    zeros = jnp.zeros_like(west0)
    west_last, _, w_last, z_last, g_end, z_first = lax.fori_loop(
        0, last, factor, (west0, ones, -ones, zeros, ones, zeros), unroll=11
    )
    prepare(last, ones)
    lower_last = -(west_last * 0.25 + half)

    columns = (
        -lower_last * w_last,
        1.0 - west_last * 0.5 - lower_last * z_last,
        west0,
        -g_end,
        z_first,
        zeros,
        zeros,
        zeros,
    )
    for at, column in enumerate(columns):
        c_s[pl.ds(8 * at, 8), :] = column
    for k in range(lev):
        c_message[k] = c_s[pl.ds(k, 8, stride=8), :]

    def shifted(i, h):
        values = [tracers[i, 8 * h + t] for t in range(8)]
        return (
            tuple(pltpu.roll(value, 1, 1) for value in values),
            tuple(pltpu.roll(value, lat - 1, 1) for value in values),
        )

    def rights(h, i, souths, norths):
        south, here, after = south_s[i], here_s[i], after_s[i]
        return [
            south * souths[t]
            + here * tracers[i, 8 * h + t]
            + (source_s[i * kinds + group[8 * h + t]] - after * norths[t])
            for t in range(8)
        ]

    def forward(h, i, carry):
        before, sums, souths, norths = carry
        low, weight = low_s[i], g_s[i]
        values, firsts = [], []
        for t, right in enumerate(rights(h, i, souths, norths)):
            value = right - low * before[t]
            plain[i, 8 * h + t] = value
            values.append(value)
            firsts.append(sums[t] + weight * value)
        return (tuple(values), tuple(firsts), *shifted(i + 1, h))

    def sweep(h):
        copies[7 + h].wait()
        nothing = (zeros,) * 8
        ends, firsts, souths, norths = lax.fori_loop(
            0, last, functools.partial(forward, h), (nothing, nothing, *shifted(0, h)), unroll=22
        )
        for t, right in enumerate(rights(h, last, souths, norths)):
            p_s[pl.ds(t * lev, lev), :] = right - lower_last * ends[t]
            q_s[pl.ds(t * lev, lev), :] = firsts[t]
        for k in range(lev):
            rows = pl.ds(k, 8, stride=lev)
            message[h, k, pl.ds(0, 8), :] = p_s[rows, :]
            message[h, k, pl.ds(8, 8), :] = q_s[rows, :]

    def send(copy_of):
        @pl.when(is_owner)
        def _():
            for step in range(1, lev):
                copy_of(lax.rem(mine + step, lev)).start()

        @pl.when(jnp.logical_not(is_owner))
        def _():
            for k in range(lev):
                copy_of(k).start()

    def settle(block, at):
        pltpu.make_async_copy(block, block, wave.at[at]).wait()

    @pl.when(is_owner)
    def _():
        pl.semaphore_wait(barrier, n - 1)

    @pl.when(jnp.logical_not(is_owner))
    def _():
        pl.semaphore_wait(barrier, lev)

    send(lambda k: early(k, me))
    for h in range(parts):
        sweep(h)
        send(lambda k: there(h, k, me))

    @pl.when(is_owner)
    def _():
        coefs[me] = c_message[mine]
        for h in range(parts):
            gathered[h, me] = message[h, mine]

    def spikes(step, carry):
        i = last - 1 - step
        w_next, v_next = carry
        ratio = ratio_s[i]
        w_here = w_ref[i] - ratio * w_next
        v_here = -ratio * v_next
        w_ref[i] = w_here
        v_ref[i] = v_here
        return w_here, v_here

    lax.fori_loop(0, last, spikes, (zeros, -ones), unroll=4)
    w_ref[last] = zeros
    v_ref[last] = -ones

    def backward(step, carry):
        i = last - 1 - step
        ratio = ratio_s[i]
        result = []
        for t in range(count):
            value = plain[i, t] - ratio * carry[t]
            plain[i, t] = value - tracers[i, t]
            result.append(value)
        return tuple(result)

    lax.fori_loop(0, last, backward, (zeros,) * count, unroll=4)
    for t in range(count):
        plain[last, t] = -tracers[last, t]

    @pl.when(is_owner)
    def _():
        others = pl.ds(0, n - 1)
        settle(coefs.at[others], 1)
        factor_levels(n, kappa, coefs, back_s)
        for h in range(parts):
            settle(gathered.at[h, others], 2 + parts + h)
            solve_level(n, h, back_s, gathered, solved)
            for step in range(n - 1):
                home(h, mine, step + jnp.where(step < me, 0, 1)).start()
            back[h, pl.ds(16 * mine, 16), :] = solved[h, pl.ds(8 * me, 16), :]

    def finish(h, owners):
        settle(back.at[h, pl.ds(0, 16 * owners)], 2 + 3 * parts + h)

    for h in range(parts):

        @pl.when(is_owner)
        def _():
            finish(h, lev - 1)

        @pl.when(jnp.logical_not(is_owner))
        def _():
            finish(h, lev)

        for j in range(2):
            for t in range(8):
                out[j, h * 8 + t] = back[h, pl.ds(j * 8 + t, lev, stride=16), :]

    def sent(owners):
        settle(c_message.at[pl.ds(0, owners)], 0)
        for h in range(parts):
            settle(message.at[h, pl.ds(0, owners)], 2 + h)

    @pl.when(is_owner)
    def _():
        sent(lev - 1)
        for h in range(parts):
            settle(gathered.at[h, pl.ds(0, n - 1)], 2 + 2 * parts + h)

    @pl.when(jnp.logical_not(is_owner))
    def _():
        sent(lev)


def combine_kernel(cuts, plain, w_s, v_s, edges, out_hbm, buffer, done):
    count = buffer.shape[1]
    parts = [pl.ds(low, high - low) for low, high in zip(cuts[:-1], cuts[1:])]
    outs = [
        pltpu.make_async_copy(buffer.at[part], out_hbm.at[part], done.at[at])
        for at, part in enumerate(parts)
    ]

    def at_cell(i, carry):
        w_here, v_here = w_s[i], v_s[i]
        for t in range(count):
            buffer[i, t] = plain[i, t] - (w_here * edges[0, t] + v_here * edges[1, t])
        return carry

    for at in range(len(parts)):
        lax.fori_loop(cuts[at], cuts[at + 1], at_cell, 0, unroll=3)
        outs[at].start()
    for copy in outs:
        copy.wait()


def on_device(tracers, zonal_flux, merid_flux, kappa, levels, groups, emissions, limiter):
    n = lax.axis_size("lon")
    cells, count, lev, lat = tracers.shape
    parts, kinds = count // 8, emissions.shape[0]
    first_owner = (n - lev) // 2
    assert lev == 8 and count % 8 == 0 and n >= lev
    f32 = jnp.float32
    hbm = pl.BlockSpec(memory_space=pl.ANY)
    vmem = pl.BlockSpec(memory_space=pltpu.VMEM)
    kappa = kappa.reshape(1, lat)
    zonal_flux, merid_flux, emissions = (
        jnp.swapaxes(value, 0, 1) for value in (zonal_flux, merid_flux, emissions)
    )
    column = (cells, lev, lat)
    levels, groups, tracers, zonal_flux, merid_flux, kappa, emissions, limiter = (
        pltpu.with_memory_space_constraint(value, pltpu.HBM)
        for value in (
            levels,
            groups,
            tracers,
            zonal_flux,
            merid_flux,
            kappa,
            emissions,
            limiter,
        )
    )
    plain, w_spike, v_spike, edges = pl.pallas_call(
        functools.partial(step_kernel, n, first_owner),
        out_shape=(
            pltpu.VMEM(tracers.shape, f32),
            pltpu.VMEM(column, f32),
            pltpu.VMEM(column, f32),
            pltpu.VMEM((2, count, lev, lat), f32),
        ),
        in_specs=[hbm] * 8,
        out_specs=(vmem,) * 4,
        scratch_shapes=[
            pltpu.SMEM(levels.shape, jnp.int32),
            pltpu.SMEM(groups.shape, jnp.int32),
            pltpu.VMEM(kappa.shape, f32),
            pltpu.VMEM(tracers.shape, f32),
            pltpu.VMEM(zonal_flux.shape, f32),
            pltpu.VMEM(merid_flux.shape, f32),
            pltpu.VMEM(emissions.shape, f32),
            pltpu.VMEM(limiter.shape, jnp.int32),
        ]
        + [pltpu.VMEM(column, f32)] * 6
        + [
            pltpu.VMEM((cells * kinds, lev, lat), f32),
            pltpu.VMEM((8 * lev, lat), f32),
            pltpu.VMEM((8 * lev, lat), f32),
            pltpu.VMEM((64, lat), f32),
            pltpu.VMEM((lev, 8, lat), f32),
            pltpu.VMEM((parts, lev, 16, lat), f32),
            pltpu.VMEM((n, 8, lat), f32),
            pltpu.VMEM((parts, n, 16, lat), f32),
            pltpu.VMEM((5, n, 8, lat), f32),
            pltpu.VMEM((parts, 8 * (n + 1), lat), f32),
            pltpu.VMEM((parts, 16 * lev, lat), f32),
            pltpu.SemaphoreType.DMA((7 + parts,)),
            pltpu.SemaphoreType.DMA((2 + 4 * parts,)),
        ],
        compiler_params=pltpu.CompilerParams(
            collective_id=0, has_side_effects=True, vmem_limit_bytes=32 << 20
        ),
        name="transport_step",
    )(levels, groups, tracers, zonal_flux, merid_flux, kappa, emissions, limiter)
    pieces = 5
    cuts = [cells * at // pieces for at in range(pieces + 1)]
    return pl.pallas_call(
        functools.partial(combine_kernel, cuts),
        out_shape=jax.ShapeDtypeStruct(tracers.shape, f32),
        in_specs=[vmem] * 4,
        out_specs=hbm,
        scratch_shapes=[
            pltpu.VMEM(tracers.shape, f32),
            pltpu.SemaphoreType.DMA((pieces,)),
        ],
        compiler_params=pltpu.CompilerParams(vmem_limit_bytes=32 << 20),
        name="combine",
    )(plain, w_spike, v_spike, edges)


def solution(mesh):
    placed = (
        P("lon", "ens", None, None),
        P("ens", "lon", None),
        P("ens", "lon", None),
        P(),
        P(),
        P(),
        P(None, "lon", None),
        P("lon", None),
    )
    return jax.shard_map(
        on_device,
        mesh=mesh,
        in_specs=placed,
        out_specs=P("lon", "ens", None, None),
        check_vma=False,
    )
```

```python
import functools

import jax
import jax.numpy as jnp
from jax import lax
from jax.experimental import pallas as pl
from jax.experimental.pallas import tpu as pltpu
from jax.sharding import PartitionSpec as P

MESH = pl.DeviceIdType.MESH


def row(ref, index):
    return jnp.broadcast_to(ref[pl.ds(index, 1), :], (8, ref.shape[-1]))


def factor_levels(n, kappa, coefs, back_s):
    half = kappa * 0.5

    def coef(d, c):
        return jnp.broadcast_to(coefs[d, pl.ds(c, 1), :], (8, kappa.shape[-1]))

    delta, z_prev = 1.0, 0.0
    ratios, zs = [], []
    for d in range(n):
        e = (d + 1) % n
        west = coef(e, 2)
        upper = west * 0.25 - half
        before = coef(d, 0)
        after = -upper * coef(e, 3)
        total = coef(d, 1) + west * 0.5 - upper * coef(e, 4)
        back_s[0, d] = upper
        if d < n - 1:
            num = total - before * delta
            inv = 1.0 / (num - after)
            delta = num * inv
            z_prev = total * inv - before * inv * z_prev
            back_s[1, d] = before * inv
            back_s[2, d] = inv
            ratio = after * inv
            back_s[3, d] = ratio
            ratios.append(ratio)
            zs.append(z_prev)
    for d in range(n - 3, -1, -1):
        zs[d] = zs[d] - ratios[d] * zs[d + 1]
    bottom = total - before * zs[n - 2] - after * zs[0]
    back_s[1, n - 1] = before
    back_s[2, n - 1] = 1.0 / bottom
    back_s[3, n - 1] = after
    for d in range(n - 1):
        back_s[4, d] = 1.0 - zs[d]


def solve_level(n, h, back_s, gathered, solved):
    top, low = pl.ds(0, 4), pl.ds(4, 4)

    def factor(c, d):
        return back_s[c, d, top, :]

    y_prev = 0.0
    ys = []
    for d in range(n):
        e = (d + 1) % n
        right = gathered[h, d, top, :] - factor(0, d) * gathered[h, e, low, :]
        if d < n - 1:
            y_prev = right * factor(2, d) - factor(1, d) * y_prev
            ys.append(y_prev)
    for d in range(n - 3, -1, -1):
        ys[d] = ys[d] - factor(3, d) * ys[d + 1]
    end = n - 1
    x_end = (right - factor(1, end) * ys[end - 1] - factor(3, end) * ys[0]) * factor(2, end)
    solved[h, 0, top, :] = x_end
    solved[h, end, low, :] = x_end
    for d in range(n - 1):
        value = ys[d] + factor(4, d) * x_end
        solved[h, d, low, :] = value
        solved[h, d + 1, top, :] = value


def step_kernel(
    n,
    first_owner,
    levels_hbm,
    groups_hbm,
    tracers_hbm,
    zonal_hbm,
    merid_hbm,
    kappa_hbm,
    emissions_hbm,
    limiter_hbm,
    plain,
    w_ref,
    v_ref,
    out,
    levels,
    groups,
    kappa_ref,
    tracers,
    zonal,
    merid,
    emissions,
    limiter,
    low_s,
    ratio_s,
    g_s,
    south_s,
    here_s,
    after_s,
    source_s,
    p_s,
    q_s,
    c_s,
    c_message,
    message,
    coefs,
    gathered,
    back_s,
    solved,
    back,
    sem,
    wave,
):
    cells, count, lev, lat = tracers.shape
    kinds = emissions.shape[1]
    parts = count // 8
    waves = count // 4
    last = cells - 1
    me = lax.axis_index("lon")
    ens = lax.axis_index("ens")
    is_owner = jnp.logical_and(me >= first_owner, me < first_owner + lev)
    mine = me - first_owner

    halves = [pl.ds(8 * h, 8) for h in range(parts)]
    copies = [
        pltpu.make_async_copy(source, target, sem.at[at])
        for at, (source, target) in enumerate(
            [
                (levels_hbm, levels),
                (kappa_hbm, kappa_ref),
                (zonal_hbm, zonal),
                (merid_hbm, merid),
                (limiter_hbm, limiter),
                (groups_hbm, groups),
                (emissions_hbm, emissions),
            ]
            + [(tracers_hbm.at[:, half], tracers.at[:, half]) for half in halves]
        )
    ]
    for copy in copies[:4]:
        copy.start()
    barrier = pltpu.get_barrier_semaphore()

    def greet(device):
        pl.semaphore_signal(barrier, inc=1, device_id=(ens, device), device_id_type=MESH)

    @pl.when(is_owner)
    def _():
        for step in range(1, n):
            greet(lax.rem(me + step, n))

    @pl.when(jnp.logical_not(is_owner))
    def _():
        for k in range(lev):
            greet(first_owner + k)

    for copy in copies[4:]:
        copy.start()

    def remote(source, target, send, recv, device):
        return pltpu.make_async_remote_copy(
            src_ref=source,
            dst_ref=target,
            send_sem=send,
            recv_sem=recv,
            device_id=(ens, device),
            device_id_type=MESH,
        )

    def early(k, sender):
        return remote(
            c_message.at[k], coefs.at[sender], wave.at[0], wave.at[1], first_owner + k
        )

    def there(h, k, sender):
        return remote(
            message.at[h, k],
            gathered.at[h, sender],
            wave.at[3],
            wave.at[4 + h],
            first_owner + k,
        )

    def home(h, k, device):
        return remote(
            solved.at[h, device],
            back.at[h, pl.ds(8 * k, 8), :],
            wave.at[2],
            wave.at[4 + waves + h],
            device,
        )

    for copy in copies[:3]:
        copy.wait()
    kappa = row(kappa_ref, 0)
    half = kappa * 0.5
    level = [levels[k] for k in range(lev)]
    lane = lax.broadcasted_iota(jnp.int32, (lev, lat), 1)
    sublane = lax.broadcasted_iota(jnp.int32, (lev, lat), 0)

    def at_cell(ref, i):
        value = jnp.broadcast_to(ref[i, pl.ds(level[0], 1), :], (lev, lat))
        for k in range(1, lev):
            other = jnp.broadcast_to(ref[i, pl.ds(level[k], 1), :], (lev, lat))
            value = jnp.where(sublane == k, other, value)
        return value

    def prepare(i, inv):
        face = jnp.where(lane > 0, at_cell(merid, i), 0.0)
        upwind = jnp.where(face > 0, 1.0, 0.0)
        share = jnp.where(row(limiter, i) == 1, upwind, 0.5)
        south = face * share
        north = face - south
        south_s[i] = south * inv
        here_s[i] = (2.0 + north - pltpu.roll(south, lat - 1, 1)) * inv
        after_s[i] = pltpu.roll(north, lat - 1, 1) * inv
        for g in range(kinds):
            value = jnp.broadcast_to(emissions[i, pl.ds(g, 1), :], (lev, lat))
            source_s[i * kinds + g] = value * inv

    def factor(i, carry):
        west, delta, w_prev, z_prev, g_here, z_first = carry
        east = at_cell(zonal, i + 1)
        lower = -(west * 0.25 + half)
        upper = east * 0.25 - half
        total = 1.0 + (east - west) * 0.5
        num = total - lower * delta
        inv = 1.0 / (num - upper)
        delta = num * inv
        low = lower * inv
        ratio = upper * inv
        w_here = -low * w_prev
        z_here = total * inv - low * z_prev
        low_s[i] = low
        ratio_s[i] = ratio
        g_s[i] = g_here
        w_ref[i] = w_here
        prepare(i, inv)
        return east, delta, w_here, z_here, -ratio * g_here, z_first + g_here * z_here

    for copy in copies[3:7]:
        copy.wait()
    group = [groups[t] for t in range(count)]
    west0 = at_cell(zonal, 0)
    ones = jnp.ones_like(west0)
    zeros = jnp.zeros_like(west0)
    west_last, _, w_last, z_last, g_end, z_first = lax.fori_loop(
        0, last, factor, (west0, ones, -ones, zeros, ones, zeros), unroll=11
    )
    prepare(last, ones)
    lower_last = -(west_last * 0.25 + half)

    columns = (
        -lower_last * w_last,
        1.0 - west_last * 0.5 - lower_last * z_last,
        west0,
        -g_end,
        z_first,
        zeros,
        zeros,
        zeros,
    )
    for at, column in enumerate(columns):
        c_s[pl.ds(8 * at, 8), :] = column
    for k in range(lev):
        c_message[k] = c_s[pl.ds(k, 8, stride=8), :]

    def shifted(i, h):
        values = [tracers[i, 4 * h + t] for t in range(4)]
        return (
            tuple(pltpu.roll(value, 1, 1) for value in values),
            tuple(pltpu.roll(value, lat - 1, 1) for value in values),
        )

    def rights(h, i, souths, norths):
        south, here, after = south_s[i], here_s[i], after_s[i]
        return [
            south * souths[t]
            + here * tracers[i, 4 * h + t]
            + (source_s[i * kinds + group[4 * h + t]] - after * norths[t])
            for t in range(4)
        ]

    def forward(h, i, carry):
        before, sums, souths, norths = carry
        low, weight = low_s[i], g_s[i]
        values, firsts = [], []
        for t, right in enumerate(rights(h, i, souths, norths)):
            value = right - low * before[t]
            plain[i, 4 * h + t] = value
            values.append(value)
            firsts.append(sums[t] + weight * value)
        return (tuple(values), tuple(firsts), *shifted(i + 1, h))

    def sweep(h):
        if h % 2 == 0:
            copies[7 + h // 2].wait()
        nothing = (zeros,) * 4
        ends, firsts, souths, norths = lax.fori_loop(
            0, last, functools.partial(forward, h), (nothing, nothing, *shifted(0, h)), unroll=22
        )
        for t, right in enumerate(rights(h, last, souths, norths)):
            p_s[pl.ds(t * lev, lev), :] = right - lower_last * ends[t]
            q_s[pl.ds(t * lev, lev), :] = firsts[t]
        for k in range(lev):
            rows = pl.ds(k, 4, stride=lev)
            message[h, k, pl.ds(0, 4), :] = p_s[rows, :]
            message[h, k, pl.ds(4, 4), :] = q_s[rows, :]

    def send(copy_of):
        @pl.when(is_owner)
        def _():
            for step in range(1, lev):
                copy_of(step - 1 + jnp.where(step - 1 < mine, 0, 1)).start()

        @pl.when(jnp.logical_not(is_owner))
        def _():
            for k in range(lev):
                copy_of(k).start()

    def settle(block, at):
        pltpu.make_async_copy(block, block, wave.at[at]).wait()

    @pl.when(is_owner)
    def _():
        pl.semaphore_wait(barrier, n - 1)

    @pl.when(jnp.logical_not(is_owner))
    def _():
        pl.semaphore_wait(barrier, lev)

    send(lambda k: early(k, me))
    for h in range(waves):
        sweep(h)
        send(lambda k: there(h, k, me))

    @pl.when(is_owner)
    def _():
        coefs[me] = c_message[mine]
        for h in range(waves):
            gathered[h, me] = message[h, mine]

    def spikes(step, carry):
        i = last - 1 - step
        w_next, v_next = carry
        ratio = ratio_s[i]
        w_here = w_ref[i] - ratio * w_next
        v_here = -ratio * v_next
        w_ref[i] = w_here
        v_ref[i] = v_here
        return w_here, v_here

    lax.fori_loop(0, last, spikes, (zeros, -ones), unroll=4)
    w_ref[last] = zeros
    v_ref[last] = -ones

    def backward(step, carry):
        i = last - 1 - step
        ratio = ratio_s[i]
        result = []
        for t in range(count):
            value = plain[i, t] - ratio * carry[t]
            plain[i, t] = value - tracers[i, t]
            result.append(value)
        return tuple(result)

    lax.fori_loop(0, last, backward, (zeros,) * count, unroll=4)
    for t in range(count):
        plain[last, t] = -tracers[last, t]

    @pl.when(is_owner)
    def _():
        others = pl.ds(0, n - 1)
        settle(coefs.at[others], 1)
        factor_levels(n, kappa, coefs, back_s)
        for h in range(waves):
            settle(gathered.at[h, others], 4 + h)
            solve_level(n, h, back_s, gathered, solved)
            for step in range(n - 1):
                home(h, mine, step + jnp.where(step < me, 0, 1)).start()
            back[h, pl.ds(8 * mine, 8), :] = solved[h, me]

    def finish(h, owners):
        settle(back.at[h, pl.ds(0, 8 * owners)], 4 + waves + h)

    for h in range(waves):

        @pl.when(is_owner)
        def _():
            finish(h, lev - 1)

        @pl.when(jnp.logical_not(is_owner))
        def _():
            finish(h, lev)

        for j in range(2):
            for t in range(4):
                out[j, h * 4 + t] = back[h, pl.ds(j * 4 + t, lev, stride=8), :]

    def sent(owners):
        settle(c_message.at[pl.ds(0, owners)], 0)
        settle(message.at[:, pl.ds(0, owners)], 3)

    @pl.when(is_owner)
    def _():
        sent(lev - 1)
        settle(gathered.at[:, pl.ds(0, n - 1)], 2)

    @pl.when(jnp.logical_not(is_owner))
    def _():
        sent(lev)


def combine_kernel(cuts, plain, w_s, v_s, edges, out_hbm, buffer, done):
    count = buffer.shape[1]
    parts = [pl.ds(low, high - low) for low, high in zip(cuts[:-1], cuts[1:])]
    outs = [
        pltpu.make_async_copy(buffer.at[part], out_hbm.at[part], done.at[at])
        for at, part in enumerate(parts)
    ]

    def at_cell(i, carry):
        w_here, v_here = w_s[i], v_s[i]
        for t in range(count):
            buffer[i, t] = plain[i, t] - (w_here * edges[0, t] + v_here * edges[1, t])
        return carry

    for at in range(len(parts)):
        lax.fori_loop(cuts[at], cuts[at + 1], at_cell, 0, unroll=3)
        outs[at].start()
    for copy in outs:
        copy.wait()


def on_device(tracers, zonal_flux, merid_flux, kappa, levels, groups, emissions, limiter):
    n = lax.axis_size("lon")
    cells, count, lev, lat = tracers.shape
    parts, waves, kinds = count // 8, count // 4, emissions.shape[0]
    first_owner = (n - lev) // 2
    assert lev == 8 and count % 8 == 0 and n >= lev
    f32 = jnp.float32
    hbm = pl.BlockSpec(memory_space=pl.ANY)
    vmem = pl.BlockSpec(memory_space=pltpu.VMEM)
    kappa = kappa.reshape(1, lat)
    zonal_flux, merid_flux, emissions = (
        jnp.swapaxes(value, 0, 1) for value in (zonal_flux, merid_flux, emissions)
    )
    column = (cells, lev, lat)
    levels, groups, tracers, zonal_flux, merid_flux, kappa, emissions, limiter = (
        pltpu.with_memory_space_constraint(value, pltpu.HBM)
        for value in (
            levels,
            groups,
            tracers,
            zonal_flux,
            merid_flux,
            kappa,
            emissions,
            limiter,
        )
    )
    plain, w_spike, v_spike, edges = pl.pallas_call(
        functools.partial(step_kernel, n, first_owner),
        out_shape=(
            pltpu.VMEM(tracers.shape, f32),
            pltpu.VMEM(column, f32),
            pltpu.VMEM(column, f32),
            pltpu.VMEM((2, count, lev, lat), f32),
        ),
        in_specs=[hbm] * 8,
        out_specs=(vmem,) * 4,
        scratch_shapes=[
            pltpu.SMEM(levels.shape, jnp.int32),
            pltpu.SMEM(groups.shape, jnp.int32),
            pltpu.VMEM(kappa.shape, f32),
            pltpu.VMEM(tracers.shape, f32),
            pltpu.VMEM(zonal_flux.shape, f32),
            pltpu.VMEM(merid_flux.shape, f32),
            pltpu.VMEM(emissions.shape, f32),
            pltpu.VMEM(limiter.shape, jnp.int32),
        ]
        + [pltpu.VMEM(column, f32)] * 6
        + [
            pltpu.VMEM((cells * kinds, lev, lat), f32),
            pltpu.VMEM((8 * lev, lat), f32),
            pltpu.VMEM((8 * lev, lat), f32),
            pltpu.VMEM((64, lat), f32),
            pltpu.VMEM((lev, 8, lat), f32),
            pltpu.VMEM((waves, lev, 8, lat), f32),
            pltpu.VMEM((n, 8, lat), f32),
            pltpu.VMEM((waves, n, 8, lat), f32),
            pltpu.VMEM((5, n, 8, lat), f32),
            pltpu.VMEM((waves, n, 8, lat), f32),
            pltpu.VMEM((waves, 8 * lev, lat), f32),
            pltpu.SemaphoreType.DMA((7 + parts,)),
            pltpu.SemaphoreType.DMA((4 + 2 * waves,)),
        ],
        compiler_params=pltpu.CompilerParams(
            collective_id=0, has_side_effects=True, vmem_limit_bytes=32 << 20
        ),
        name="transport_step",
    )(levels, groups, tracers, zonal_flux, merid_flux, kappa, emissions, limiter)
    pieces = 5
    cuts = [cells * at // pieces for at in range(pieces + 1)]
    return pl.pallas_call(
        functools.partial(combine_kernel, cuts),
        out_shape=jax.ShapeDtypeStruct(tracers.shape, f32),
        in_specs=[vmem] * 4,
        out_specs=hbm,
        scratch_shapes=[
            pltpu.VMEM(tracers.shape, f32),
            pltpu.SemaphoreType.DMA((pieces,)),
        ],
        compiler_params=pltpu.CompilerParams(vmem_limit_bytes=32 << 20),
        name="combine",
    )(plain, w_spike, v_spike, edges)


def solution(mesh):
    placed = (
        P("lon", "ens", None, None),
        P("ens", "lon", None),
        P("ens", "lon", None),
        P(),
        P(),
        P(),
        P(None, "lon", None),
        P("lon", None),
    )
    return jax.shard_map(
        on_device,
        mesh=mesh,
        in_specs=placed,
        out_specs=P("lon", "ens", None, None),
        check_vma=False,
    )
```

```python
import functools

import jax
import jax.numpy as jnp
from jax import lax
from jax.experimental import pallas as pl
from jax.experimental.pallas import tpu as pltpu
from jax.sharding import PartitionSpec as P

MESH = pl.DeviceIdType.MESH


def row(ref, index):
    return jnp.broadcast_to(ref[pl.ds(index, 1), :], (8, ref.shape[-1]))


def factor_levels(n, kappa, coefs, back_s):
    half = kappa * 0.5

    def coef(d, c):
        return jnp.broadcast_to(coefs[d, pl.ds(c, 1), :], (8, kappa.shape[-1]))

    delta, z_prev = 1.0, 0.0
    ratios, zs = [], []
    for d in range(n):
        e = (d + 1) % n
        west = coef(e, 2)
        upper = west * 0.25 - half
        before = coef(d, 0)
        after = -upper * coef(e, 3)
        total = coef(d, 1) + west * 0.5 - upper * coef(e, 4)
        back_s[0, d] = upper
        if d < n - 1:
            num = total - before * delta
            inv = 1.0 / (num - after)
            delta = num * inv
            z_prev = total * inv - before * inv * z_prev
            back_s[1, d] = before * inv
            back_s[2, d] = inv
            ratio = after * inv
            back_s[3, d] = ratio
            ratios.append(ratio)
            zs.append(z_prev)
    for d in range(n - 3, -1, -1):
        zs[d] = zs[d] - ratios[d] * zs[d + 1]
    bottom = total - before * zs[n - 2] - after * zs[0]
    back_s[1, n - 1] = before
    back_s[2, n - 1] = 1.0 / bottom
    back_s[3, n - 1] = after
    for d in range(n - 1):
        back_s[4, d] = 1.0 - zs[d]


def solve_level(n, h, back_s, gathered, solved):
    top, low = pl.ds(0, 4), pl.ds(4, 4)

    def factor(c, d):
        return back_s[c, d, top, :]

    y_prev = 0.0
    ys = []
    for d in range(n):
        e = (d + 1) % n
        right = gathered[h, d, top, :] - factor(0, d) * gathered[h, e, low, :]
        if d < n - 1:
            y_prev = right * factor(2, d) - factor(1, d) * y_prev
            ys.append(y_prev)
    for d in range(n - 3, -1, -1):
        ys[d] = ys[d] - factor(3, d) * ys[d + 1]
    end = n - 1
    x_end = (right - factor(1, end) * ys[end - 1] - factor(3, end) * ys[0]) * factor(2, end)
    solved[h, 0, top, :] = x_end
    solved[h, end, low, :] = x_end
    for d in range(n - 1):
        value = ys[d] + factor(4, d) * x_end
        solved[h, d, low, :] = value
        solved[h, d + 1, top, :] = value


def step_kernel(
    n,
    first_owner,
    levels_hbm,
    groups_hbm,
    tracers_hbm,
    zonal_hbm,
    merid_hbm,
    kappa_hbm,
    emissions_hbm,
    limiter_hbm,
    plain,
    w_ref,
    v_ref,
    out,
    levels,
    groups,
    kappa_ref,
    tracers,
    zonal,
    merid,
    emissions,
    limiter,
    low_s,
    ratio_s,
    g_s,
    south_s,
    here_s,
    after_s,
    source_s,
    p_s,
    q_s,
    c_s,
    c_message,
    message,
    coefs,
    gathered,
    back_s,
    solved,
    back,
    sem,
    wave,
):
    cells, count, lev, lat = tracers.shape
    kinds = emissions.shape[1]
    parts = count // 8
    waves = count // 4
    prompt = min(4, first_owner)
    last = cells - 1
    me = lax.axis_index("lon")
    ens = lax.axis_index("ens")
    is_owner = jnp.logical_and(me >= first_owner, me < first_owner + lev)
    mine = me - first_owner

    halves = [pl.ds(8 * h, 8) for h in range(parts)]
    copies = [
        pltpu.make_async_copy(source, target, sem.at[at])
        for at, (source, target) in enumerate(
            [
                (levels_hbm, levels),
                (kappa_hbm, kappa_ref),
                (zonal_hbm, zonal),
                (merid_hbm, merid),
                (limiter_hbm, limiter),
                (groups_hbm, groups),
                (emissions_hbm, emissions),
            ]
            + [(tracers_hbm.at[:, half], tracers.at[:, half]) for half in halves]
        )
    ]
    for copy in copies[:4]:
        copy.start()
    barrier = pltpu.get_barrier_semaphore()

    def greet(device):
        pl.semaphore_signal(barrier, inc=1, device_id=(ens, device), device_id_type=MESH)

    @pl.when(is_owner)
    def _():
        for step in range(1, n):
            greet(lax.rem(me + step, n))

    for copy in copies[4:]:
        copy.start()

    def remote(source, target, send, recv, device):
        return pltpu.make_async_remote_copy(
            src_ref=source,
            dst_ref=target,
            send_sem=send,
            recv_sem=recv,
            device_id=(ens, device),
            device_id_type=MESH,
        )

    def early(k, sender):
        return remote(
            c_message.at[k], coefs.at[sender], wave.at[0], wave.at[1], first_owner + k
        )

    def there(h, k, sender):
        return remote(
            message.at[h, k],
            gathered.at[h, sender],
            wave.at[3],
            wave.at[4 + h],
            first_owner + k,
        )

    def home(h, k, device):
        return remote(
            solved.at[h, device],
            back.at[h, pl.ds(8 * k, 8), :],
            wave.at[2],
            wave.at[4 + waves + h],
            device,
        )

    def rest(k, device):
        return remote(
            solved.at[:, device],
            back.at[:, pl.ds(8 * k, 8), :],
            wave.at[2],
            wave.at[4 + waves],
            device,
        )

    for copy in copies[:3]:
        copy.wait()
    kappa = row(kappa_ref, 0)
    half = kappa * 0.5
    level = [levels[k] for k in range(lev)]
    lane = lax.broadcasted_iota(jnp.int32, (lev, lat), 1)
    sublane = lax.broadcasted_iota(jnp.int32, (lev, lat), 0)

    def at_cell(ref, i):
        value = jnp.broadcast_to(ref[i, pl.ds(level[0], 1), :], (lev, lat))
        for k in range(1, lev):
            other = jnp.broadcast_to(ref[i, pl.ds(level[k], 1), :], (lev, lat))
            value = jnp.where(sublane == k, other, value)
        return value

    def prepare(i, inv):
        face = jnp.where(lane > 0, at_cell(merid, i), 0.0)
        upwind = jnp.where(face > 0, 1.0, 0.0)
        share = jnp.where(row(limiter, i) == 1, upwind, 0.5)
        south = face * share
        north = face - south
        south_s[i] = south * inv
        here_s[i] = (2.0 + north - pltpu.roll(south, lat - 1, 1)) * inv
        after_s[i] = pltpu.roll(north, lat - 1, 1) * inv
        for g in range(kinds):
            value = jnp.broadcast_to(emissions[i, pl.ds(g, 1), :], (lev, lat))
            source_s[i * kinds + g] = value * inv

    def factor(i, carry):
        west, delta, w_prev, z_prev, g_here, z_first = carry
        east = at_cell(zonal, i + 1)
        lower = -(west * 0.25 + half)
        upper = east * 0.25 - half
        total = 1.0 + (east - west) * 0.5
        num = total - lower * delta
        inv = 1.0 / (num - upper)
        delta = num * inv
        low = lower * inv
        ratio = upper * inv
        w_here = -low * w_prev
        z_here = total * inv - low * z_prev
        low_s[i] = low
        ratio_s[i] = ratio
        g_s[i] = g_here
        w_ref[i] = w_here
        prepare(i, inv)
        return east, delta, w_here, z_here, -ratio * g_here, z_first + g_here * z_here

    for copy in copies[3:7]:
        copy.wait()
    group = [groups[t] for t in range(count)]
    west0 = at_cell(zonal, 0)
    ones = jnp.ones_like(west0)
    zeros = jnp.zeros_like(west0)
    west_last, _, w_last, z_last, g_end, z_first = lax.fori_loop(
        0, last, factor, (west0, ones, -ones, zeros, ones, zeros), unroll=11
    )
    prepare(last, ones)
    lower_last = -(west_last * 0.25 + half)

    columns = (
        -lower_last * w_last,
        1.0 - west_last * 0.5 - lower_last * z_last,
        west0,
        -g_end,
        z_first,
        zeros,
        zeros,
        zeros,
    )
    for at, column in enumerate(columns):
        c_s[pl.ds(8 * at, 8), :] = column
    for k in range(lev):
        c_message[k] = c_s[pl.ds(k, 8, stride=8), :]

    def shifted(i, h):
        values = [tracers[i, 4 * h + t] for t in range(4)]
        return (
            tuple(pltpu.roll(value, 1, 1) for value in values),
            tuple(pltpu.roll(value, lat - 1, 1) for value in values),
        )

    def rights(h, i, souths, norths):
        south, here, after = south_s[i], here_s[i], after_s[i]
        return [
            south * souths[t]
            + here * tracers[i, 4 * h + t]
            + (source_s[i * kinds + group[4 * h + t]] - after * norths[t])
            for t in range(4)
        ]

    def forward(h, i, carry):
        before, sums, souths, norths = carry
        low, weight = low_s[i], g_s[i]
        values, firsts = [], []
        for t, right in enumerate(rights(h, i, souths, norths)):
            value = right - low * before[t]
            plain[i, 4 * h + t] = value
            values.append(value)
            firsts.append(sums[t] + weight * value)
        return (tuple(values), tuple(firsts), *shifted(i + 1, h))

    def sweep(h):
        if h % 2 == 0:
            copies[7 + h // 2].wait()
        nothing = (zeros,) * 4
        ends, firsts, souths, norths = lax.fori_loop(
            0, last, functools.partial(forward, h), (nothing, nothing, *shifted(0, h)), unroll=22
        )
        for t, right in enumerate(rights(h, last, souths, norths)):
            p_s[pl.ds(t * lev, lev), :] = right - lower_last * ends[t]
            q_s[pl.ds(t * lev, lev), :] = firsts[t]
        for k in range(lev):
            rows = pl.ds(k, 4, stride=lev)
            message[h, k, pl.ds(0, 4), :] = p_s[rows, :]
            message[h, k, pl.ds(4, 4), :] = q_s[rows, :]

    def send(copy_of):
        @pl.when(is_owner)
        def _():
            for step in range(1, lev):
                copy_of(step - 1 + jnp.where(step - 1 < mine, 0, 1)).start()

        @pl.when(jnp.logical_not(is_owner))
        def _():
            for k in range(lev):
                copy_of(k).start()

    def settle(block, at):
        pltpu.make_async_copy(block, block, wave.at[at]).wait()

    @pl.when(is_owner)
    def _():
        pl.semaphore_wait(barrier, lev - 1)

    @pl.when(jnp.logical_not(is_owner))
    def _():
        pl.semaphore_wait(barrier, lev)

    send(lambda k: early(k, me))
    for h in range(waves):
        sweep(h)
        send(lambda k: there(h, k, me))

    @pl.when(is_owner)
    def _():
        coefs[me] = c_message[mine]
        for h in range(waves):
            gathered[h, me] = message[h, mine]

    def spikes(step, carry):
        i = last - 1 - step
        w_next, v_next = carry
        ratio = ratio_s[i]
        w_here = w_ref[i] - ratio * w_next
        v_here = -ratio * v_next
        w_ref[i] = w_here
        v_ref[i] = v_here
        return w_here, v_here

    lax.fori_loop(0, last, spikes, (zeros, -ones), unroll=4)
    w_ref[last] = zeros
    v_ref[last] = -ones

    def backward(step, carry):
        i = last - 1 - step
        ratio = ratio_s[i]
        result = []
        for t in range(count):
            value = plain[i, t] - ratio * carry[t]
            plain[i, t] = value - tracers[i, t]
            result.append(value)
        return tuple(result)

    lax.fori_loop(0, last, backward, (zeros,) * count, unroll=4)
    for t in range(count):
        plain[last, t] = -tracers[last, t]

    @pl.when(is_owner)
    def _():
        others = pl.ds(0, n - 1)
        settle(coefs.at[others], 1)
        factor_levels(n, kappa, coefs, back_s)
        for h in range(waves):
            settle(gathered.at[h, others], 4 + h)
            solve_level(n, h, back_s, gathered, solved)
            for device in range(prompt):
                home(h, mine, device).start()
            back[h, pl.ds(8 * mine, 8), :] = solved[h, me]
        for step in range(prompt, n - 1):
            rest(mine, step + jnp.where(step < me, 0, 1)).start()
        settle(back.at[:, pl.ds(0, 8 * (lev - 1))], 4 + waves)

    @pl.when(me < prompt)
    def _():
        for h in range(waves):
            settle(back.at[h, pl.ds(0, 8 * lev)], 4 + waves + h)

    @pl.when(jnp.logical_and(me >= prompt, jnp.logical_not(is_owner)))
    def _():
        settle(back.at[:, pl.ds(0, 8 * lev)], 4 + waves)

    for h in range(waves):
        for j in range(2):
            for t in range(4):
                out[j, h * 4 + t] = back[h, pl.ds(j * 4 + t, lev, stride=8), :]

    def sent(owners):
        settle(c_message.at[pl.ds(0, owners)], 0)
        settle(message.at[:, pl.ds(0, owners)], 3)

    @pl.when(is_owner)
    def _():
        sent(lev - 1)
        settle(gathered.at[:, pl.ds(0, n - 1)], 2)

    @pl.when(jnp.logical_not(is_owner))
    def _():
        sent(lev)


def combine_kernel(cuts, plain, w_s, v_s, edges, out_hbm, buffer, done):
    count = buffer.shape[1]
    parts = [pl.ds(low, high - low) for low, high in zip(cuts[:-1], cuts[1:])]
    outs = [
        pltpu.make_async_copy(buffer.at[part], out_hbm.at[part], done.at[at])
        for at, part in enumerate(parts)
    ]

    def at_cell(i, carry):
        w_here, v_here = w_s[i], v_s[i]
        for t in range(count):
            buffer[i, t] = plain[i, t] - (w_here * edges[0, t] + v_here * edges[1, t])
        return carry

    for at in range(len(parts)):
        lax.fori_loop(cuts[at], cuts[at + 1], at_cell, 0, unroll=3)
        outs[at].start()
    for copy in outs:
        copy.wait()


def on_device(tracers, zonal_flux, merid_flux, kappa, levels, groups, emissions, limiter):
    n = lax.axis_size("lon")
    cells, count, lev, lat = tracers.shape
    parts, waves, kinds = count // 8, count // 4, emissions.shape[0]
    first_owner = (n - lev) // 2
    assert lev == 8 and count % 8 == 0 and n >= lev
    f32 = jnp.float32
    hbm = pl.BlockSpec(memory_space=pl.ANY)
    vmem = pl.BlockSpec(memory_space=pltpu.VMEM)
    kappa = kappa.reshape(1, lat)
    zonal_flux, merid_flux, emissions = (
        jnp.swapaxes(value, 0, 1) for value in (zonal_flux, merid_flux, emissions)
    )
    column = (cells, lev, lat)
    levels, groups, tracers, zonal_flux, merid_flux, kappa, emissions, limiter = (
        pltpu.with_memory_space_constraint(value, pltpu.HBM)
        for value in (
            levels,
            groups,
            tracers,
            zonal_flux,
            merid_flux,
            kappa,
            emissions,
            limiter,
        )
    )
    plain, w_spike, v_spike, edges = pl.pallas_call(
        functools.partial(step_kernel, n, first_owner),
        out_shape=(
            pltpu.VMEM(tracers.shape, f32),
            pltpu.VMEM(column, f32),
            pltpu.VMEM(column, f32),
            pltpu.VMEM((2, count, lev, lat), f32),
        ),
        in_specs=[hbm] * 8,
        out_specs=(vmem,) * 4,
        scratch_shapes=[
            pltpu.SMEM(levels.shape, jnp.int32),
            pltpu.SMEM(groups.shape, jnp.int32),
            pltpu.VMEM(kappa.shape, f32),
            pltpu.VMEM(tracers.shape, f32),
            pltpu.VMEM(zonal_flux.shape, f32),
            pltpu.VMEM(merid_flux.shape, f32),
            pltpu.VMEM(emissions.shape, f32),
            pltpu.VMEM(limiter.shape, jnp.int32),
        ]
        + [pltpu.VMEM(column, f32)] * 6
        + [
            pltpu.VMEM((cells * kinds, lev, lat), f32),
            pltpu.VMEM((8 * lev, lat), f32),
            pltpu.VMEM((8 * lev, lat), f32),
            pltpu.VMEM((64, lat), f32),
            pltpu.VMEM((lev, 8, lat), f32),
            pltpu.VMEM((waves, lev, 8, lat), f32),
            pltpu.VMEM((n, 8, lat), f32),
            pltpu.VMEM((waves, n, 8, lat), f32),
            pltpu.VMEM((5, n, 8, lat), f32),
            pltpu.VMEM((waves, n, 8, lat), f32),
            pltpu.VMEM((waves, 8 * lev, lat), f32),
            pltpu.SemaphoreType.DMA((7 + parts,)),
            pltpu.SemaphoreType.DMA((4 + 2 * waves,)),
        ],
        compiler_params=pltpu.CompilerParams(
            collective_id=0, has_side_effects=True, vmem_limit_bytes=32 << 20
        ),
        name="transport_step",
    )(levels, groups, tracers, zonal_flux, merid_flux, kappa, emissions, limiter)
    pieces = 5
    cuts = [cells * at // pieces for at in range(pieces + 1)]
    return pl.pallas_call(
        functools.partial(combine_kernel, cuts),
        out_shape=jax.ShapeDtypeStruct(tracers.shape, f32),
        in_specs=[vmem] * 4,
        out_specs=hbm,
        scratch_shapes=[
            pltpu.VMEM(tracers.shape, f32),
            pltpu.SemaphoreType.DMA((pieces,)),
        ],
        compiler_params=pltpu.CompilerParams(vmem_limit_bytes=32 << 20),
        name="combine",
    )(plain, w_spike, v_spike, edges)


def solution(mesh):
    placed = (
        P("lon", "ens", None, None),
        P("ens", "lon", None),
        P("ens", "lon", None),
        P(),
        P(),
        P(),
        P(None, "lon", None),
        P("lon", None),
    )
    return jax.shard_map(
        on_device,
        mesh=mesh,
        in_specs=placed,
        out_specs=P("lon", "ens", None, None),
        check_vma=False,
    )
```

```python
import functools

import jax
import jax.numpy as jnp
from jax import lax
from jax.experimental import pallas as pl
from jax.experimental.pallas import tpu as pltpu
from jax.sharding import PartitionSpec as P

MESH = pl.DeviceIdType.MESH


def row(ref, index):
    return jnp.broadcast_to(ref[pl.ds(index, 1), :], (8, ref.shape[-1]))


def factor_levels(n, kappa, coefs, back_s):
    half = kappa * 0.5

    def coef(d, c):
        return jnp.broadcast_to(coefs[d, pl.ds(c, 1), :], (8, kappa.shape[-1]))

    delta, z_prev = 1.0, 0.0
    ratios, zs = [], []
    for d in range(n):
        e = (d + 1) % n
        west = coef(e, 2)
        upper = west * 0.25 - half
        before = coef(d, 0)
        after = -upper * coef(e, 3)
        total = coef(d, 1) + west * 0.5 - upper * coef(e, 4)
        back_s[0, d] = upper
        if d < n - 1:
            num = total - before * delta
            inv = 1.0 / (num - after)
            delta = num * inv
            z_prev = total * inv - before * inv * z_prev
            back_s[1, d] = before * inv
            back_s[2, d] = inv
            ratio = after * inv
            back_s[3, d] = ratio
            ratios.append(ratio)
            zs.append(z_prev)
    for d in range(n - 3, -1, -1):
        zs[d] = zs[d] - ratios[d] * zs[d + 1]
    bottom = total - before * zs[n - 2] - after * zs[0]
    back_s[1, n - 1] = before
    back_s[2, n - 1] = 1.0 / bottom
    back_s[3, n - 1] = after
    for d in range(n - 1):
        back_s[4, d] = 1.0 - zs[d]


def solve_level(n, h, back_s, gathered, solved):
    top, low = pl.ds(0, 4), pl.ds(4, 4)

    def factor(c, d):
        return back_s[c, d, top, :]

    y_prev = 0.0
    ys = []
    for d in range(n):
        e = (d + 1) % n
        right = gathered[h, d, top, :] - factor(0, d) * gathered[h, e, low, :]
        if d < n - 1:
            y_prev = right * factor(2, d) - factor(1, d) * y_prev
            ys.append(y_prev)
    for d in range(n - 3, -1, -1):
        ys[d] = ys[d] - factor(3, d) * ys[d + 1]
    end = n - 1
    x_end = (right - factor(1, end) * ys[end - 1] - factor(3, end) * ys[0]) * factor(2, end)
    solved[h, 0, top, :] = x_end
    solved[h, end, low, :] = x_end
    for d in range(n - 1):
        value = ys[d] + factor(4, d) * x_end
        solved[h, d, low, :] = value
        solved[h, d + 1, top, :] = value


def step_kernel(
    n,
    first_owner,
    levels_hbm,
    groups_hbm,
    tracers_hbm,
    zonal_hbm,
    merid_hbm,
    kappa_hbm,
    emissions_hbm,
    limiter_hbm,
    plain,
    w_ref,
    v_ref,
    out,
    levels,
    groups,
    kappa_ref,
    tracers,
    zonal,
    merid,
    emissions,
    limiter,
    low_s,
    ratio_s,
    g_s,
    south_s,
    here_s,
    after_s,
    source_s,
    p_s,
    q_s,
    c_s,
    c_message,
    message,
    coefs,
    gathered,
    back_s,
    solved,
    back,
    sem,
    wave,
):
    cells, count, lev, lat = tracers.shape
    kinds = emissions.shape[1]
    parts = count // 8
    waves = count // 4
    prompt = min(4, first_owner)
    last = cells - 1
    me = lax.axis_index("lon")
    ens = lax.axis_index("ens")
    is_owner = jnp.logical_and(me >= first_owner, me < first_owner + lev)
    mine = me - first_owner

    halves = [pl.ds(8 * h, 8) for h in range(parts)]
    copies = [
        pltpu.make_async_copy(source, target, sem.at[at])
        for at, (source, target) in enumerate(
            [
                (levels_hbm, levels),
                (kappa_hbm, kappa_ref),
                (zonal_hbm, zonal),
                (merid_hbm, merid),
                (limiter_hbm, limiter),
                (groups_hbm, groups),
                (emissions_hbm, emissions),
            ]
            + [(tracers_hbm.at[:, half], tracers.at[:, half]) for half in halves]
        )
    ]
    for copy in copies[:4]:
        copy.start()
    barrier = pltpu.get_barrier_semaphore()

    def greet(device):
        pl.semaphore_signal(barrier, inc=1, device_id=(ens, device), device_id_type=MESH)

    @pl.when(is_owner)
    def _():
        for step in range(1, n):
            greet(lax.rem(me + step, n))

    for copy in copies[4:]:
        copy.start()

    def remote(source, target, send, recv, device):
        return pltpu.make_async_remote_copy(
            src_ref=source,
            dst_ref=target,
            send_sem=send,
            recv_sem=recv,
            device_id=(ens, device),
            device_id_type=MESH,
        )

    def early(k, sender):
        return remote(
            c_message.at[k, pl.ds(0, 5)], coefs.at[sender, pl.ds(0, 5)], wave.at[0], wave.at[1], first_owner + k
        )

    def there(h, k, sender):
        return remote(
            message.at[h, k],
            gathered.at[h, sender],
            wave.at[3],
            wave.at[4 + h],
            first_owner + k,
        )

    def home(h, k, device):
        return remote(
            solved.at[h, device],
            back.at[h, pl.ds(8 * k, 8), :],
            wave.at[2],
            wave.at[4 + waves + h],
            device,
        )

    def rest(k, device):
        return remote(
            solved.at[:, device],
            back.at[:, pl.ds(8 * k, 8), :],
            wave.at[2],
            wave.at[4 + waves],
            device,
        )

    for copy in copies[:3]:
        copy.wait()
    kappa = row(kappa_ref, 0)
    half = kappa * 0.5
    level = [levels[k] for k in range(lev)]
    lane = lax.broadcasted_iota(jnp.int32, (lev, lat), 1)
    sublane = lax.broadcasted_iota(jnp.int32, (lev, lat), 0)

    def at_cell(ref, i):
        value = jnp.broadcast_to(ref[i, pl.ds(level[0], 1), :], (lev, lat))
        for k in range(1, lev):
            other = jnp.broadcast_to(ref[i, pl.ds(level[k], 1), :], (lev, lat))
            value = jnp.where(sublane == k, other, value)
        return value

    def prepare(i, inv):
        face = jnp.where(lane > 0, at_cell(merid, i), 0.0)
        upwind = jnp.where(face > 0, 1.0, 0.0)
        share = jnp.where(row(limiter, i) == 1, upwind, 0.5)
        south = face * share
        north = face - south
        south_s[i] = south * inv
        here_s[i] = (2.0 + north - pltpu.roll(south, lat - 1, 1)) * inv
        after_s[i] = pltpu.roll(north, lat - 1, 1) * inv
        for g in range(kinds):
            value = jnp.broadcast_to(emissions[i, pl.ds(g, 1), :], (lev, lat))
            source_s[i * kinds + g] = value * inv

    def factor(i, carry):
        west, delta, w_prev, z_prev, g_here, z_first = carry
        east = at_cell(zonal, i + 1)
        lower = -(west * 0.25 + half)
        upper = east * 0.25 - half
        total = 1.0 + (east - west) * 0.5
        num = total - lower * delta
        inv = 1.0 / (num - upper)
        delta = num * inv
        low = lower * inv
        ratio = upper * inv
        w_here = -low * w_prev
        z_here = total * inv - low * z_prev
        low_s[i] = low
        ratio_s[i] = ratio
        g_s[i] = g_here
        w_ref[i] = w_here
        prepare(i, inv)
        return east, delta, w_here, z_here, -ratio * g_here, z_first + g_here * z_here

    for copy in copies[3:7]:
        copy.wait()
    group = [groups[t] for t in range(count)]
    west0 = at_cell(zonal, 0)
    ones = jnp.ones_like(west0)
    zeros = jnp.zeros_like(west0)
    west_last, _, w_last, z_last, g_end, z_first = lax.fori_loop(
        0, last, factor, (west0, ones, -ones, zeros, ones, zeros), unroll=11
    )
    prepare(last, ones)
    lower_last = -(west_last * 0.25 + half)

    columns = (
        -lower_last * w_last,
        1.0 - west_last * 0.5 - lower_last * z_last,
        west0,
        -g_end,
        z_first,
        zeros,
        zeros,
        zeros,
    )
    for at, column in enumerate(columns):
        c_s[pl.ds(8 * at, 8), :] = column
    for k in range(lev):
        c_message[k] = c_s[pl.ds(k, 8, stride=8), :]

    def shifted(i, h):
        values = [tracers[i, 4 * h + t] for t in range(4)]
        return (
            tuple(pltpu.roll(value, 1, 1) for value in values),
            tuple(pltpu.roll(value, lat - 1, 1) for value in values),
        )

    def rights(h, i, souths, norths):
        south, here, after = south_s[i], here_s[i], after_s[i]
        return [
            south * souths[t]
            + here * tracers[i, 4 * h + t]
            + (source_s[i * kinds + group[4 * h + t]] - after * norths[t])
            for t in range(4)
        ]

    def forward(h, i, carry):
        before, sums, souths, norths = carry
        low, weight = low_s[i], g_s[i]
        values, firsts = [], []
        for t, right in enumerate(rights(h, i, souths, norths)):
            value = right - low * before[t]
            plain[i, 4 * h + t] = value
            values.append(value)
            firsts.append(sums[t] + weight * value)
        return (tuple(values), tuple(firsts), *shifted(i + 1, h))

    def sweep(h):
        if h % 2 == 0:
            copies[7 + h // 2].wait()
        nothing = (zeros,) * 4
        ends, firsts, souths, norths = lax.fori_loop(
            0, last, functools.partial(forward, h), (nothing, nothing, *shifted(0, h)), unroll=22
        )
        for t, right in enumerate(rights(h, last, souths, norths)):
            p_s[pl.ds(t * lev, lev), :] = right - lower_last * ends[t]
            q_s[pl.ds(t * lev, lev), :] = firsts[t]
        for k in range(lev):
            rows = pl.ds(k, 4, stride=lev)
            message[h, k, pl.ds(0, 4), :] = p_s[rows, :]
            message[h, k, pl.ds(4, 4), :] = q_s[rows, :]

    def send(copy_of):
        @pl.when(is_owner)
        def _():
            for step in range(1, lev):
                copy_of(step - 1 + jnp.where(step - 1 < mine, 0, 1)).start()

        @pl.when(jnp.logical_not(is_owner))
        def _():
            for k in range(lev):
                copy_of(k).start()

    def settle(block, at):
        pltpu.make_async_copy(block, block, wave.at[at]).wait()

    @pl.when(is_owner)
    def _():
        pl.semaphore_wait(barrier, lev - 1)

    @pl.when(jnp.logical_not(is_owner))
    def _():
        pl.semaphore_wait(barrier, lev)

    send(lambda k: early(k, me))
    for h in range(waves):
        sweep(h)
        send(lambda k: there(h, k, me))

    @pl.when(is_owner)
    def _():
        coefs[me] = c_message[mine]
        for h in range(waves):
            gathered[h, me] = message[h, mine]

    def spikes(step, carry):
        i = last - 1 - step
        w_next, v_next = carry
        ratio = ratio_s[i]
        w_here = w_ref[i] - ratio * w_next
        v_here = -ratio * v_next
        w_ref[i] = w_here
        v_ref[i] = v_here
        return w_here, v_here

    lax.fori_loop(0, last, spikes, (zeros, -ones), unroll=4)
    w_ref[last] = zeros
    v_ref[last] = -ones

    def backward(step, carry):
        i = last - 1 - step
        ratio = ratio_s[i]
        result = []
        for t in range(count):
            value = plain[i, t] - ratio * carry[t]
            plain[i, t] = value - tracers[i, t]
            result.append(value)
        return tuple(result)

    lax.fori_loop(0, last, backward, (zeros,) * count, unroll=4)
    for t in range(count):
        plain[last, t] = -tracers[last, t]

    @pl.when(is_owner)
    def _():
        others = pl.ds(0, n - 1)
        settle(coefs.at[others, pl.ds(0, 5)], 1)
        factor_levels(n, kappa, coefs, back_s)
        for h in range(waves):
            settle(gathered.at[h, others], 4 + h)
            solve_level(n, h, back_s, gathered, solved)
            for device in range(prompt):
                home(h, mine, device).start()
            back[h, pl.ds(8 * mine, 8), :] = solved[h, me]
        for step in range(prompt, n - 1):
            rest(mine, step + jnp.where(step < me, 0, 1)).start()
        settle(back.at[:, pl.ds(0, 8 * (lev - 1))], 4 + waves)

    @pl.when(me < prompt)
    def _():
        for h in range(waves):
            settle(back.at[h, pl.ds(0, 8 * lev)], 4 + waves + h)

    @pl.when(jnp.logical_and(me >= prompt, jnp.logical_not(is_owner)))
    def _():
        settle(back.at[:, pl.ds(0, 8 * lev)], 4 + waves)

    for h in range(waves):
        for j in range(2):
            for t in range(4):
                out[j, h * 4 + t] = back[h, pl.ds(j * 4 + t, lev, stride=8), :]

    def sent(owners):
        settle(c_message.at[pl.ds(0, owners), pl.ds(0, 5)], 0)
        settle(message.at[:, pl.ds(0, owners)], 3)

    @pl.when(is_owner)
    def _():
        sent(lev - 1)
        settle(gathered.at[:, pl.ds(0, n - 1)], 2)

    @pl.when(jnp.logical_not(is_owner))
    def _():
        sent(lev)


def combine_kernel(cuts, plain, w_s, v_s, edges, out_hbm, buffer, done):
    count = buffer.shape[1]
    parts = [pl.ds(low, high - low) for low, high in zip(cuts[:-1], cuts[1:])]
    outs = [
        pltpu.make_async_copy(buffer.at[part], out_hbm.at[part], done.at[at])
        for at, part in enumerate(parts)
    ]

    def at_cell(i, carry):
        w_here, v_here = w_s[i], v_s[i]
        for t in range(count):
            buffer[i, t] = plain[i, t] - (w_here * edges[0, t] + v_here * edges[1, t])
        return carry

    for at in range(len(parts)):
        lax.fori_loop(cuts[at], cuts[at + 1], at_cell, 0, unroll=3)
        outs[at].start()
    for copy in outs:
        copy.wait()


def on_device(tracers, zonal_flux, merid_flux, kappa, levels, groups, emissions, limiter):
    n = lax.axis_size("lon")
    cells, count, lev, lat = tracers.shape
    parts, waves, kinds = count // 8, count // 4, emissions.shape[0]
    first_owner = (n - lev) // 2
    assert lev == 8 and count % 8 == 0 and n >= lev
    f32 = jnp.float32
    hbm = pl.BlockSpec(memory_space=pl.ANY)
    vmem = pl.BlockSpec(memory_space=pltpu.VMEM)
    kappa = kappa.reshape(1, lat)
    zonal_flux, merid_flux, emissions = (
        jnp.swapaxes(value, 0, 1) for value in (zonal_flux, merid_flux, emissions)
    )
    column = (cells, lev, lat)
    levels, groups, tracers, zonal_flux, merid_flux, kappa, emissions, limiter = (
        pltpu.with_memory_space_constraint(value, pltpu.HBM)
        for value in (
            levels,
            groups,
            tracers,
            zonal_flux,
            merid_flux,
            kappa,
            emissions,
            limiter,
        )
    )
    plain, w_spike, v_spike, edges = pl.pallas_call(
        functools.partial(step_kernel, n, first_owner),
        out_shape=(
            pltpu.VMEM(tracers.shape, f32),
            pltpu.VMEM(column, f32),
            pltpu.VMEM(column, f32),
            pltpu.VMEM((2, count, lev, lat), f32),
        ),
        in_specs=[hbm] * 8,
        out_specs=(vmem,) * 4,
        scratch_shapes=[
            pltpu.SMEM(levels.shape, jnp.int32),
            pltpu.SMEM(groups.shape, jnp.int32),
            pltpu.VMEM(kappa.shape, f32),
            pltpu.VMEM(tracers.shape, f32),
            pltpu.VMEM(zonal_flux.shape, f32),
            pltpu.VMEM(merid_flux.shape, f32),
            pltpu.VMEM(emissions.shape, f32),
            pltpu.VMEM(limiter.shape, jnp.int32),
        ]
        + [pltpu.VMEM(column, f32)] * 6
        + [
            pltpu.VMEM((cells * kinds, lev, lat), f32),
            pltpu.VMEM((8 * lev, lat), f32),
            pltpu.VMEM((8 * lev, lat), f32),
            pltpu.VMEM((64, lat), f32),
            pltpu.VMEM((lev, 8, lat), f32),
            pltpu.VMEM((waves, lev, 8, lat), f32),
            pltpu.VMEM((n, 8, lat), f32),
            pltpu.VMEM((waves, n, 8, lat), f32),
            pltpu.VMEM((5, n, 8, lat), f32),
            pltpu.VMEM((waves, n, 8, lat), f32),
            pltpu.VMEM((waves, 8 * lev, lat), f32),
            pltpu.SemaphoreType.DMA((7 + parts,)),
            pltpu.SemaphoreType.DMA((4 + 2 * waves,)),
        ],
        compiler_params=pltpu.CompilerParams(
            collective_id=0, has_side_effects=True, vmem_limit_bytes=32 << 20
        ),
        name="transport_step",
    )(levels, groups, tracers, zonal_flux, merid_flux, kappa, emissions, limiter)
    pieces = 5
    cuts = [cells * at // pieces for at in range(pieces + 1)]
    return pl.pallas_call(
        functools.partial(combine_kernel, cuts),
        out_shape=jax.ShapeDtypeStruct(tracers.shape, f32),
        in_specs=[vmem] * 4,
        out_specs=hbm,
        scratch_shapes=[
            pltpu.VMEM(tracers.shape, f32),
            pltpu.SemaphoreType.DMA((pieces,)),
        ],
        compiler_params=pltpu.CompilerParams(vmem_limit_bytes=32 << 20),
        name="combine",
    )(plain, w_spike, v_spike, edges)


def solution(mesh):
    placed = (
        P("lon", "ens", None, None),
        P("ens", "lon", None),
        P("ens", "lon", None),
        P(),
        P(),
        P(),
        P(None, "lon", None),
        P("lon", None),
    )
    return jax.shard_map(
        on_device,
        mesh=mesh,
        in_specs=placed,
        out_specs=P("lon", "ens", None, None),
        check_vma=False,
    )
```
